512 devices in a mesh: row: 64 (over z, y_hi, x), col: 8 (over y_lo, core).
Axes of the slice: x: 4, y: 8 (y_hi: 2, y_lo: 4; y = y_hi * 4 + y_lo), z: 8, core: 2. Of those that a mesh axis runs over, the one named last changes fastest.
Arguments:
- a_tiles: bfloat16 [4096, 48, 64, 64], P('row', 'col'), may hold values from -4 to 4
- a_cols: int32 [4096, 48], P('row', 'col'), may hold values from 0 to 511
- a_count: int32 [4096, 8], P('row', 'col'), may hold values from 1 to 6
- a_slot: int32 [4096, 48], P('row', 'col'), may hold values from 0 to 26
- agg: int32 [4096], P('row'), may hold values from 0 to 3
- p_tiles: bfloat16 [8, 512, 64, 64], P('col', 'row'), may hold values from -0.75 to 0.75
Outputs:
- coarse: float32 [128, 27, 64, 64], P('row', None, 'col')
The draws below stay inside these ranges and needn't reach their ends.
All inputs are finite; a program needn't handle non-finite values.
Results may differ from the reference program's by a relative error of at most 0.0065.
Values may be sent and summed in bfloat16 or wider, within the bound.
No kernel may reach another device: no remote copies, remote signals or barrier semaphores. Data moves between devices by JAX's collectives and lax.ppermute only.
A program may use at most 128 MiB of HBM per device.

```python
import jax
import jax.numpy as jnp
from jax import lax

TILE = 64
BR = 64
KA = 6
KC = 27
CR = 2
NF = 4096
BC = 512
NC = 128
N_ROW = 64
N_COL = 8


def plant(values, key, smallest, high):
    longest = values.shape.index(max(values.shape))
    spots = []
    for shift in (0, 1):
        where = [jax.random.randint(jax.random.fold_in(key, axis), (), 0, length) for axis, length in enumerate(values.shape)]
        where[longest] = (where[longest] + shift) % values.shape[longest]
        spots.append(tuple(where))
    return values.at[spots[0]].set(smallest).at[spots[1]].set(high)


def level_of(stream_key, extent, shards, least, top_value):
    factor_of = 1.0
    for position, shards_of in shards:
        steps = jax.random.uniform(jax.random.fold_in(jax.random.fold_in(stream_key, 6), position), (shards_of,), jnp.float32, least / len(shards), top_value / len(shards))
        factor_of = factor_of * jnp.repeat(jnp.exp(steps), extent[position] // shards_of).reshape((-1,) + (1,) * (len(extent) - 1 - position))
    return factor_of


def scatter_about(key, shape, scale, bound, shards=(), kind=jnp.bfloat16):
    values = scale * jax.random.normal(key, shape, jnp.float32)
    if shards:
        values = values * level_of(key, shape, shards, -0.22, 0.18)
    return jnp.clip(values, -bound, bound).astype(kind)


def setup_inputs(seed: int = 0) -> dict:
    streams_of = jax.random.split(jax.random.key(seed), 7)
    a_tiles = scatter_about(streams_of[0], (NF, N_COL * KA, TILE, TILE), 0.25, 4.0, ((0, 64), (1, 8)))
    a_cols = plant(jax.random.randint(streams_of[1], (NF, N_COL * KA), 0, BC), jax.random.fold_in(streams_of[1], 1), 0, BC - 1).astype(jnp.int32)
    a_count = plant(jax.random.randint(streams_of[2], (NF, N_COL), 1, KA + 1), jax.random.fold_in(streams_of[2], 1), 1, KA).astype(jnp.int32)
    a_slot = plant(jax.random.randint(streams_of[3], (NF, N_COL * KA), 0, KC), jax.random.fold_in(streams_of[3], 1), 0, KC - 1).astype(jnp.int32)
    agg = plant(jax.random.randint(streams_of[4], (NF,), 0, 2 * CR), jax.random.fold_in(streams_of[4], 1), 0, (2 * CR) - 1).astype(jnp.int32)
    p_tiles = scatter_about(streams_of[5], (N_COL, BC, TILE, TILE), TILE ** -0.5, 0.75, ((0, 8), (1, 64)))
    return {"a_tiles": a_tiles, "a_cols": a_cols, "a_count": a_count, "a_slot": a_slot, "agg": agg, "p_tiles": p_tiles}


def reference(a_tiles, a_cols, a_count, a_slot, agg, p_tiles):
    width = N_COL * KA
    panel_of = (jnp.arange(width, dtype=jnp.int32) // KA).astype(jnp.int32)
    slot_of = (jnp.arange(width, dtype=jnp.int32) % KA).astype(jnp.int32)
    total = NC * KC

    def one_panel(carry, panel):
        first = (panel * BR).astype(jnp.int32)
        blocks = lax.dynamic_slice_in_dim(a_tiles, first, BR, 0)
        columns = lax.dynamic_slice_in_dim(a_cols, first, BR, 0)
        counts = lax.dynamic_slice_in_dim(a_count, first, BR, 0)
        slots = lax.dynamic_slice_in_dim(a_slot, first, BR, 0)
        groups = lax.dynamic_slice_in_dim(agg, first, BR, 0)
        chosen = p_tiles[panel_of[None, :], columns]
        product = jnp.einsum("bkxy,bkyz->bkxz", blocks.astype(jnp.float32), chosen.astype(jnp.float32)).astype(jnp.bfloat16)
        fine = first + jnp.arange(BR, dtype=jnp.int32)
        own_p = p_tiles[fine % N_COL, fine // N_COL]
        term = jnp.einsum("byx,bkyz->bkxz", own_p.astype(jnp.float32), product.astype(jnp.float32))
        live = slot_of[None, :] < counts[:, panel_of]
        term = term * live[:, :, None, None].astype(jnp.float32)
        target = (panel * CR + groups) % NC
        dest = (target[:, None] * KC + slots).reshape(-1)
        added = jax.ops.segment_sum(term.reshape(BR * width, TILE, TILE), dest, num_segments=total)
        return carry + added, None

    start = jnp.zeros((total, TILE, TILE), jnp.float32)
    result, _ = lax.scan(one_panel, start, jnp.arange(N_ROW, dtype=jnp.int32))
    return result.reshape(NC, KC, TILE, TILE)
```

```python
import jax
import jax.numpy as jnp
from jax import lax
from jax.experimental import pallas as pl
from jax.experimental.pallas import tpu as pltpu
from jax.sharding import Mesh, PartitionSpec as P

KC = 27
CR = 2
T = 64
NY = 4
ROW = ("z", "yh", "x")
COL = ("yl", "core")
UNROLL = 8
F32 = jnp.float32
BF16 = jnp.bfloat16


def spread(value, axis):
    count = lax.axis_size(axis)
    copies = jnp.broadcast_to(value[None], (count,) + value.shape)
    return lax.all_to_all(copies, axis, 0, 0, tiled=True)


def left_kernel(own_ref, a_ref, b_ref):
    for c in range(8):
        both = own_ref[c, 0].astype(F32).T.astype(BF16)
        for h in range(2):
            left = both[h * T:(h + 1) * T]
            for s in range(a_ref.shape[3]):
                b_ref[h, 0, c, s] = jnp.dot(left, a_ref[h, 0, c, s], preferred_element_type=F32).astype(BF16)


def left_products(own, a_tiles):
    rows, slots = a_tiles.shape[:2]
    a = a_tiles.reshape(2, 4, 8, slots, T, T)
    b = pl.pallas_call(
        left_kernel,
        grid=(4,),
        in_specs=[
            pl.BlockSpec((8, 1, T, 2 * T), lambda v: (0, v, 0, 0)),
            pl.BlockSpec((2, 1, 8, slots, T, T), lambda v: (0, v, 0, 0, 0, 0)),
        ],
        out_specs=pl.BlockSpec((2, 1, 8, slots, T, T), lambda v: (0, v, 0, 0, 0, 0)),
        out_shape=jax.ShapeDtypeStruct(a.shape, BF16),
        compiler_params=pltpu.CompilerParams(vmem_limit_bytes=40 * 2**20),
        cost_estimate=pl.CostEstimate(flops=2 * rows * slots * T**3, bytes_accessed=16 * 2**20, transcendentals=0),
        name="left_products",
    )(own, a)
    return b.reshape(rows * slots, T, T)


def sum_kernel(which_ref, pair_ref, into_ref, info_ref, panel_ref, b_ref, out_ref, acc):
    core = info_ref[1]

    @pl.loop(0, acc.shape[0] // 2)
    def _(d):
        for e in range(2):
            acc[2 * d + e] = jnp.zeros((T, 2 * T), F32)

    @pl.loop(0, (info_ref[0] + UNROLL - 1) // UNROLL)
    def _(step):
        for half in range(2):
            base = step * UNROLL + half * (UNROLL // 2)
            terms = [
                jnp.dot(b_ref[which_ref[base + e]], panel_ref[pair_ref[base + e]], preferred_element_type=F32)
                for e in range(UNROLL // 2)
            ]
            for e in range(UNROLL // 2):
                d = into_ref[base + e]
                acc[d] = acc[d] + terms[e]

    low = lax.broadcasted_iota(jnp.int32, (T, 2 * T), 1) < T

    @pl.loop(0, KC)
    def _(k):
        parts = []
        for p in range(2):
            d0 = 2 * ((2 * p) * KC + k)
            d1 = 2 * ((2 * p + 1) * KC + k)
            parts.append(jnp.where(low, acc[d0], acc[d1 + 1]) + pltpu.roll(jnp.where(low, acc[d1], acc[d0 + 1]), T, 1))
        for o in range(8):
            tile = jnp.concatenate([parts[0][o * 8:(o + 1) * 8], parts[1][o * 8:(o + 1) * 8]], axis=0)
            out_ref[jnp.bitwise_xor(core, o % 2), o // 2, k] = tile.astype(BF16)


def panel_sums(which, pair, into, info, panel, b):
    slots = b.shape[0]
    smem = pl.BlockSpec(memory_space=pltpu.SMEM)
    vmem = pl.BlockSpec(memory_space=pltpu.VMEM)
    return pl.pallas_call(
        sum_kernel,
        in_specs=[smem, smem, smem, smem, vmem, vmem],
        out_specs=vmem,
        out_shape=jax.ShapeDtypeStruct((2, NY, KC, 16, 2 * T), BF16),
        scratch_shapes=[pltpu.VMEM((2 * (2 * CR * KC + 1), T, 2 * T), F32)],
        compiler_params=pltpu.CompilerParams(vmem_limit_bytes=40 * 2**20),
        cost_estimate=pl.CostEstimate(flops=4 * slots * T**3, bytes_accessed=16 * 2**20, transcendentals=0),
        name="panel_sums",
    )(which, pair, into, info, panel, b)


def body(a_tiles, a_cols, a_count, a_slot, agg, p_tiles):
    rows, slots = a_tiles.shape[:2]
    total = rows * slots
    packed = jnp.concatenate([p_tiles[0, :4], p_tiles[0, 4:]], axis=-1)

    own = spread(packed, COL)
    near = spread(packed, ("yh", "x"))
    panel = lax.all_gather(near, "z", axis=0, tiled=False).reshape(-1, T, 2 * T)

    live = (jnp.arange(slots, dtype=jnp.int32)[None, :] < a_count).reshape(total)
    before = jnp.cumsum(live.astype(jnp.int32)) - 1
    n_live = before[-1] + 1
    here = (before[None, :] == jnp.arange(total, dtype=jnp.int32)[:, None]) & live[None, :]

    def front(value, fill):
        value = value.reshape(total)
        kept = jnp.sum(jnp.where(here, value[None, :], 0), axis=1)
        return jnp.where(jnp.arange(total) < n_live, kept, fill).astype(jnp.int32)

    which = front(jnp.arange(total, dtype=jnp.int32), 0)
    pair = front((a_cols // 8) * 4 + a_cols % 4, 0)
    target = 2 * (agg[:, None] * KC + a_slot) + (a_cols % 8) // 4
    into = front(target, 2 * 2 * CR * KC)
    info = jnp.stack([n_live, lax.axis_index("core")]).astype(jnp.int32)

    b = left_products(own, a_tiles)
    sums = panel_sums(which, pair, into, info, panel, b)
    other = lax.ppermute(sums[1], "core", [(0, 1), (1, 0)])
    chip = (sums[0].astype(F32) + other.astype(F32)).astype(BF16)
    shares = lax.all_to_all(chip, "yl", 0, 0, tiled=True)
    done = jnp.sum(shares.astype(F32), axis=0)
    count = lax.axis_size(ROW)
    moved = lax.ppermute(done[:, 8:].astype(BF16), ROW, [(i, (i + 1) % count) for i in range(count)])
    result = done[:, :8] + moved.astype(F32)
    return jnp.stack([result[..., :T], result[..., T:]])


def solution(mesh):
    fine = Mesh(mesh.devices.reshape(8, 2, 4, 4, 2), ROW + COL)
    return jax.shard_map(
        body,
        mesh=fine,
        in_specs=(
            P(ROW, COL, None, None),
            P(ROW, COL),
            P(ROW, COL),
            P(ROW, COL),
            P(ROW),
            P(COL, ROW, None, None),
        ),
        out_specs=P(ROW, None, COL, None),
        check_vma=False,
    )
```

```python
import functools

import jax
import jax.numpy as jnp
from jax import lax
from jax.experimental import pallas as pl
from jax.experimental.pallas import tpu as pltpu
from jax.sharding import Mesh, PartitionSpec as P

KC = 27
KP = 28
CR = 2
T = 64
NY = 4
HALF = CR * KC
ROW = ("z", "yh", "x")
COL = ("yl", "core")
UNROLL = 8
F32 = jnp.float32
BF16 = jnp.bfloat16
I32 = jnp.int32
MIB = 2**20


def shifted(value, axis, by):
    count = lax.axis_size(axis)
    return lax.ppermute(value, axis, [(i, (i + by) % count) for i in range(count)])


def spread(value, axis):
    count = lax.axis_size(axis)
    copies = jnp.broadcast_to(value[None], (count,) + value.shape)
    return lax.all_to_all(copies, axis, 0, 0, tiled=True)


def left_kernel(info_ref, own_ref, a_ref, b_ref):
    core = info_ref[8]
    for c in range(8):
        both = own_ref[c // 2, jnp.bitwise_xor(core, c % 2), 0].astype(F32).T.astype(BF16)
        for h in range(2):
            left = both[h * T:(h + 1) * T]
            for s in range(a_ref.shape[3]):
                b_ref[h, 0, c, s] = jnp.dot(left, a_ref[h, 0, c, s], preferred_element_type=F32).astype(BF16)


def left_products(info, own, a_tiles):
    rows, slots = a_tiles.shape[:2]
    a = a_tiles.reshape(2, 4, 8, slots, T, T)
    b = pl.pallas_call(
        left_kernel,
        grid=(4,),
        in_specs=[
            pl.BlockSpec(memory_space=pltpu.SMEM),
            pl.BlockSpec((4, 2, 1, T, 2 * T), lambda v: (0, 0, v, 0, 0)),
            pl.BlockSpec((2, 1, 8, slots, T, T), lambda v: (0, v, 0, 0, 0, 0)),
        ],
        out_specs=pl.BlockSpec((2, 1, 8, slots, T, T), lambda v: (0, v, 0, 0, 0, 0)),
        out_shape=jax.ShapeDtypeStruct(a.shape, BF16),
        compiler_params=pltpu.CompilerParams(vmem_limit_bytes=16 * MIB),
        cost_estimate=pl.CostEstimate(flops=2 * rows * slots * T**3, bytes_accessed=16 * MIB, transcendentals=0),
        name="left_products",
    )(info, own, a)
    return b.reshape(rows * slots, T, T)


def sum_kernel(group, sides, n_chunks, n_before, *refs):
    code_ref, info_ref = refs[:2]
    chunks = refs[2:2 + n_chunks]
    b_ref = refs[2 + n_chunks]
    before = refs[3 + n_chunks:3 + n_chunks + n_before * len(sides)]
    outs = refs[3 + n_chunks + n_before * len(sides):-3]
    panel, acc, sems = refs[-3:]
    core = info_ref[8]
    copies, at = [], 0
    for n, chunk in enumerate(chunks):
        size = chunk.shape[0]
        copies.append(pltpu.make_async_copy(chunk, panel.at[pl.ds(at, size)], sems.at[n]))
        at += size
    for copy in copies:
        copy.start()

    @pl.loop(0, acc.shape[0] // 2)
    def _(d):
        for e in range(2):
            acc[2 * d + e] = jnp.zeros((T, 2 * T), F32)

    for copy in copies:
        copy.wait()
    first = info_ref[group]

    @pl.loop(0, info_ref[4 + group])
    def _(step):
        for half in range(2):
            base = first + step * UNROLL + half * (UNROLL // 2)
            codes = [code_ref[base + e] for e in range(UNROLL // 2)]
            terms = [
                jnp.dot(
                    b_ref[jnp.bitwise_and(code, 511)],
                    panel[jnp.bitwise_and(jnp.right_shift(code, 9), 127)],
                    preferred_element_type=F32,
                )
                for code in codes
            ]
            for code, term in zip(codes, terms):
                d = jnp.right_shift(code, 16)
                acc[d] = acc[d] + term

    low = lax.broadcasted_iota(I32, (T, 2 * T), 1) < T

    @pl.loop(0, KP // 2)
    def _(m):
        for n in range(len(sides)):
            values = []
            for e in range(2):
                d0 = 2 * (n * HALF + 2 * m + e)
                d1 = d0 + 2 * KC
                values.append(
                    jnp.where(low, acc[d0], acc[d1 + 1]) + pltpu.roll(jnp.where(low, acc[d1], acc[d0 + 1]), T, 1)
                )
            for o in range(8):
                tile = jnp.concatenate([v[o * 8:(o + 1) * 8] for v in values], axis=0)
                place = (jnp.bitwise_xor(core, o % 2), o // 2, m)
                for q in range(n_before):
                    tile = tile + before[q * len(sides) + n][place].astype(F32)
                outs[n][place] = tile.astype(BF16)


def panel_sums(group, sides, code, info, chunks, b, before=()):
    smem = pl.BlockSpec(memory_space=pltpu.SMEM)
    vmem = pl.BlockSpec(memory_space=pltpu.VMEM)
    anyw = pl.BlockSpec(memory_space=pl.ANY)
    n = len(sides)
    shape = jax.ShapeDtypeStruct((2, NY, KP // 2, 16, 2 * T), BF16)
    pairs = sum(c.shape[0] for c in chunks)
    return pl.pallas_call(
        functools.partial(sum_kernel, group, sides, len(chunks), len(before) // n),
        in_specs=[smem, smem] + [anyw] * len(chunks) + [vmem] * (1 + len(before)),
        out_specs=[vmem] * n,
        out_shape=[shape] * n,
        scratch_shapes=[
            pltpu.VMEM((pairs, T, 2 * T), BF16),
            pltpu.VMEM((2 * (n * HALF + 1), T, 2 * T), F32),
            pltpu.SemaphoreType.DMA((len(chunks),)),
        ],
        compiler_params=pltpu.CompilerParams(vmem_limit_bytes=24 * MIB),
        cost_estimate=pl.CostEstimate(flops=pairs * 2**20, bytes_accessed=8 * MIB, transcendentals=0),
        name=f"panel_sums_{group}",
    )(code, info, *chunks, b, *before)


def body(a_tiles, a_cols, a_count, a_slot, agg, p_tiles):
    rows, slots = a_tiles.shape[:2]
    total = rows * slots
    core, me_x = lax.axis_index("core"), lax.axis_index("x")
    packed = jnp.concatenate([p_tiles[0, :4], p_tiles[0, 4:]], axis=-1)

    column = spread(packed, ("yh", "z")).reshape(-1, T, 2 * T)
    half = column.shape[0] // 2
    left1, right1 = shifted(column, "x", 1), shifted(column, "x", -1)

    both = jnp.stack([packed, shifted(packed, "core", 1)])
    both, _ = lax.optimization_barrier((both, column))
    own = spread(both, "yl")
    left1, right1, own = lax.optimization_barrier((left1, right1, own))
    left2, right2 = shifted(left1[:half], "x", 1), shifted(right1[half:], "x", -1)

    live = jnp.arange(slots, dtype=I32)[None, :] < a_count
    owner = a_cols // 8
    far = jnp.bitwise_and(owner - me_x + 4, 3)
    pair = ((owner // 4) % 2 * 8 + owner // 8) * 4 + a_cols % 4 + jnp.where(far == 1, 64, 0)
    side = jnp.broadcast_to(agg[:, None] // CR, a_cols.shape)
    group = jnp.where(far == 0, 0, jnp.where(far == 2, 3 - side, 1))
    target = 2 * (agg[:, None] * KC + a_slot) + (a_cols % 8) // 4
    target = jnp.where((group == 2), target - 2 * HALF, target)
    code = jnp.left_shift(target, 16) + jnp.left_shift(pair, 9) + jnp.arange(total, dtype=I32).reshape(rows, slots)
    code = code.reshape(total)
    picked = (group.reshape(total)[:, None] == jnp.arange(4, dtype=I32)) & live.reshape(total)[:, None]
    lower = jnp.arange(total, dtype=I32)[:, None] > jnp.arange(total, dtype=I32)[None, :]
    rank = jnp.dot(lower.astype(BF16), picked.astype(BF16), preferred_element_type=F32).astype(I32)
    steps = (jnp.sum(picked.astype(I32), axis=0) + UNROLL - 1) // UNROLL
    first = (jnp.cumsum(steps) - steps) * UNROLL
    place = jnp.sum(jnp.where(picked, rank + first[None, :] + 1, 0), axis=1) - 1
    spots = jnp.arange(total + 4 * UNROLL, dtype=I32)
    here = spots[:, None] == place[None, :]
    empty = jnp.left_shift(jnp.where(spots < first[2], 4 * HALF, 2 * HALF), 16)
    code = jnp.where(jnp.any(here, axis=1), jnp.sum(jnp.where(here, code[None, :], 0), axis=1), empty)
    info = jnp.concatenate([first, steps, core[None]]).astype(I32)

    b = left_products(info, own, a_tiles)
    sums0 = panel_sums(0, (0, 1), code, info, [column], b)
    sums1 = panel_sums(1, (0, 1), code, info, [left1, right1], b)
    (next2,) = panel_sums(2, (1,), code, info, [left2, right2], b, (sums0[1], sums1[1]))
    (own2,) = panel_sums(3, (0,), code, info, [left2, right2], b, (sums0[0], sums1[0]))

    def over_col(value):
        other = shifted(value[1], "core", 1)
        chip = (value[0].astype(F32) + other.astype(F32)).astype(BF16)
        return jnp.sum(lax.all_to_all(chip, "yl", 0, 0, tiled=True).astype(F32), axis=0)

    moved = shifted(over_col(next2).astype(BF16), ROW, 1)
    result = (over_col(own2) + moved.astype(F32)).reshape(KP, 8, 2 * T)[:KC]
    return jnp.stack([result[..., :T], result[..., T:]])


def solution(mesh):
    fine = Mesh(mesh.devices.reshape(8, 2, 4, 4, 2), ROW + COL)
    return jax.shard_map(
        body,
        mesh=fine,
        in_specs=(
            P(ROW, COL, None, None),
            P(ROW, COL),
            P(ROW, COL),
            P(ROW, COL),
            P(ROW),
            P(COL, ROW, None, None),
        ),
        out_specs=P(ROW, None, COL, None),
        check_vma=False,
    )
```

```python
import functools

import jax
import jax.numpy as jnp
from jax import lax
from jax.experimental import pallas as pl
from jax.experimental.pallas import tpu as pltpu
from jax.sharding import Mesh, PartitionSpec as P

KC = 27
CR = 2
T = 64
NY = 4
ROW = ("z", "yh", "x")
COL = ("yl", "core")
UNROLL = 8
F32 = jnp.float32
BF16 = jnp.bfloat16
I32 = jnp.int32
MIB = 2**20


def shifted(value, axis, by):
    count = lax.axis_size(axis)
    return lax.ppermute(value, axis, [(i, (i + by) % count) for i in range(count)])


def spread(value, axis):
    count = lax.axis_size(axis)
    copies = jnp.broadcast_to(value[None], (count,) + value.shape)
    return lax.all_to_all(copies, axis, 0, 0, tiled=True)


def left_kernel(info_ref, own_ref, a_ref, b_ref):
    core, yl = info_ref[6], info_ref[7]
    for c in range(8):
        far = jnp.bitwise_and(yl - c // 2 + NY, NY - 1)
        both = own_ref[jnp.bitwise_xor(core, c % 2), far, 0].astype(F32).T.astype(BF16)
        for h in range(2):
            left = both[h * T:(h + 1) * T]
            for s in range(a_ref.shape[3]):
                b_ref[h, 0, c, s] = jnp.dot(left, a_ref[h, 0, c, s], preferred_element_type=F32).astype(BF16)


def left_products(info, own, a_tiles):
    rows, slots = a_tiles.shape[:2]
    a = a_tiles.reshape(2, 4, 8, slots, T, T)
    b = pl.pallas_call(
        left_kernel,
        grid=(4,),
        in_specs=[
            pl.BlockSpec(memory_space=pltpu.SMEM),
            pl.BlockSpec((2, NY, 1, T, 2 * T), lambda v: (0, 0, v, 0, 0)),
            pl.BlockSpec((2, 1, 8, slots, T, T), lambda v: (0, v, 0, 0, 0, 0)),
        ],
        out_specs=pl.BlockSpec((2, 1, 8, slots, T, T), lambda v: (0, v, 0, 0, 0, 0)),
        out_shape=jax.ShapeDtypeStruct(a.shape, BF16),
        compiler_params=pltpu.CompilerParams(vmem_limit_bytes=16 * MIB),
        cost_estimate=pl.CostEstimate(flops=2 * rows * slots * T**3, bytes_accessed=16 * MIB, transcendentals=0),
        name="left_products",
    )(info, own, a)
    return b.reshape(rows * slots, T, T)


def sum_kernel(group, n_chunks, n_before, *refs):
    code_ref, info_ref = refs[:2]
    chunks = refs[2:2 + n_chunks]
    b_ref = refs[2 + n_chunks]
    before = refs[3 + n_chunks:3 + n_chunks + n_before]
    out_ref, panel, acc, sems = refs[-4:]
    core = info_ref[6]
    copies, at = [], 0
    for n, chunk in enumerate(chunks):
        size = chunk.shape[0]
        copies.append(pltpu.make_async_copy(chunk, panel.at[pl.ds(at, size)], sems.at[n]))
        at += size
    for copy in copies:
        copy.start()

    @pl.loop(0, acc.shape[0])
    def _(d):
        acc[d] = jnp.zeros((T, 2 * T), F32)

    for copy in copies:
        copy.wait()
    first = info_ref[group]
    low = lax.broadcasted_iota(I32, (T, 2 * T), 1) < T

    def placed(code):
        pairs = panel[jnp.bitwise_and(jnp.right_shift(code, 9), 127)].astype(F32)
        swap = jnp.bitwise_and(jnp.right_shift(code, 16), 1) == 1
        to_low = jnp.bitwise_and(jnp.right_shift(code, 17), 1) == 0
        pairs = jnp.where(swap, pltpu.roll(pairs, T, 1), pairs)
        return jnp.where(low == to_low, pairs, 0.0).astype(BF16)

    @pl.loop(0, info_ref[3 + group])
    def _(step):
        for half in range(2):
            base = first + step * UNROLL + half * (UNROLL // 2)
            codes = [code_ref[base + e] for e in range(UNROLL // 2)]
            terms = [
                jnp.dot(b_ref[jnp.bitwise_and(code, 511)], placed(code), preferred_element_type=F32)
                for code in codes
            ]
            for code, term in zip(codes, terms):
                d = jnp.right_shift(code, 18)
                acc[d] = acc[d] + term

    @pl.loop(0, KC)
    def _(k):
        for o in range(8):
            tile = jnp.concatenate([acc[k, o * 8:(o + 1) * 8], acc[KC + k, o * 8:(o + 1) * 8]], axis=0)
            place = (jnp.bitwise_xor(core, o % 2), o // 2, k)
            for earlier in before:
                tile = tile + earlier[place].astype(F32)
            out_ref[place] = tile.astype(BF16)


def panel_sums(group, code, info, chunks, b, before=()):
    smem = pl.BlockSpec(memory_space=pltpu.SMEM)
    vmem = pl.BlockSpec(memory_space=pltpu.VMEM)
    anyw = pl.BlockSpec(memory_space=pl.ANY)
    pairs = sum(c.shape[0] for c in chunks)
    return pl.pallas_call(
        functools.partial(sum_kernel, group, len(chunks), len(before)),
        in_specs=[smem, smem] + [anyw] * len(chunks) + [vmem] * (1 + len(before)),
        out_specs=vmem,
        out_shape=jax.ShapeDtypeStruct((2, NY, KC, 16, 2 * T), BF16),
        scratch_shapes=[
            pltpu.VMEM((pairs, T, 2 * T), BF16),
            pltpu.VMEM((2 * KC + 1, T, 2 * T), F32),
            pltpu.SemaphoreType.DMA((len(chunks),)),
        ],
        compiler_params=pltpu.CompilerParams(vmem_limit_bytes=24 * MIB),
        cost_estimate=pl.CostEstimate(flops=pairs * 2**20, bytes_accessed=8 * MIB, transcendentals=0),
        name=f"panel_sums_{group}",
    )(code, info, *chunks, b, *before)


def body(a_tiles, a_cols, a_count, a_slot, agg, p_tiles):
    rows, slots = a_tiles.shape[:2]
    total = rows * slots
    core, yl, me_x = lax.axis_index("core"), lax.axis_index("yl"), lax.axis_index("x")
    packed = jnp.concatenate([p_tiles[0, :4], p_tiles[0, 4:]], axis=-1)

    column = spread(packed, ("yh", "z"))
    own = jnp.stack([packed] + [shifted(packed, "yl", k) for k in range(1, NY)])
    column, own = lax.optimization_barrier((column, own))
    column = column.reshape(2, -1, T, 2 * T)

    left_a, right_b = shifted(column[0], "x", 1), shifted(column[1], "x", -1)
    left_b, right_a = shifted(column[1], "x", 1), shifted(column[0], "x", -1)
    left2, right2 = shifted(left_a, "x", 1), shifted(right_b, "x", -1)
    own = jnp.stack([own, shifted(own, "core", 1)])

    live = jnp.arange(slots, dtype=I32)[None, :] < a_count
    owner = a_cols // 8
    far = jnp.bitwise_and(owner - me_x + 4, 3)
    pair = ((owner // 4) % 2 * 8 + owner // 8) * 4 + a_cols % 4 + jnp.where(far == 1, 64, 0)
    group = jnp.where(far == 0, 0, jnp.where(far == 2, 2, 1))
    to_high = jnp.broadcast_to(agg[:, None] % CR, a_cols.shape)
    target = agg[:, None] // CR * KC + a_slot
    swap = ((a_cols % 8) // 4 + to_high) % 2
    code = ((target * 2 + to_high) * 2 + swap) * 2**16 + pair * 2**9 + jnp.arange(total, dtype=I32).reshape(rows, slots)
    code = code.reshape(total)
    picked = (group.reshape(total)[:, None] == jnp.arange(3, dtype=I32)) & live.reshape(total)[:, None]
    lower = jnp.arange(total, dtype=I32)[:, None] > jnp.arange(total, dtype=I32)[None, :]
    rank = jnp.dot(lower.astype(BF16), picked.astype(BF16), preferred_element_type=F32).astype(I32)
    steps = (jnp.sum(picked.astype(I32), axis=0) + UNROLL - 1) // UNROLL
    first = (jnp.cumsum(steps) - steps) * UNROLL
    place = jnp.sum(jnp.where(picked, rank + first[None, :] + 1, 0), axis=1) - 1
    here = jnp.arange(total + 3 * UNROLL, dtype=I32)[:, None] == place[None, :]
    empty = 2 * KC * 2**18
    code = jnp.sum(jnp.where(here, code[None, :] - empty, 0), axis=1) + empty
    info = jnp.concatenate([first, steps, jnp.stack([core, yl])]).astype(I32)

    b = left_products(info, own, a_tiles)
    sums0 = panel_sums(0, code, info, [column.reshape(-1, T, 2 * T)], b)
    sums1 = panel_sums(1, code, info, [left_a, left_b, right_a, right_b], b)
    sums2 = panel_sums(2, code, info, [left2, right2], b, (sums0, sums1))

    chip = (sums2[0].astype(F32) + shifted(sums2[1], "core", 1).astype(F32)).astype(BF16)
    shares = jnp.sum(lax.all_to_all(chip, "yl", 0, 0, tiled=True).astype(F32), axis=0)
    moved = shifted(shares[:, 8:].astype(BF16), ROW, 1)
    result = shares[:, :8] + moved.astype(F32)
    return jnp.stack([result[..., :T], result[..., T:]])


def solution(mesh):
    fine = Mesh(mesh.devices.reshape(8, 2, 4, 4, 2), ROW + COL)
    return jax.shard_map(
        body,
        mesh=fine,
        in_specs=(
            P(ROW, COL, None, None),
            P(ROW, COL),
            P(ROW, COL),
            P(ROW, COL),
            P(ROW),
            P(COL, ROW, None, None),
        ),
        out_specs=P(ROW, None, COL, None),
        check_vma=False,
    )
```

```python
import functools

import jax
import jax.numpy as jnp
from jax import lax
from jax.experimental import pallas as pl
from jax.experimental.pallas import tpu as pltpu
from jax.sharding import Mesh, PartitionSpec as P

KC = 27
CR = 2
T = 64
NY = 4
ROW = ("z", "yh", "x")
COL = ("yl", "core")
UNROLL = 8
F32 = jnp.float32
BF16 = jnp.bfloat16
I32 = jnp.int32
MIB = 2**20


def shifted(value, axis, by):
    count = lax.axis_size(axis)
    return lax.ppermute(value, axis, [(i, (i + by) % count) for i in range(count)])


def spread(value, axis):
    count = lax.axis_size(axis)
    copies = jnp.broadcast_to(value[None], (count,) + value.shape)
    return lax.all_to_all(copies, axis, 0, 0, tiled=True)


def left_kernel(info_ref, own_ref, a_ref, b_ref, done_ref, a_here, sems):
    core, yl = info_ref[6], info_ref[7]
    done_ref[...] = jnp.zeros(done_ref.shape, F32)

    def fetch(v, h):
        return pltpu.make_async_copy(a_ref.at[h, v], a_here.at[v, h], sems.at[v, h])

    for v in range(4):
        for h in range(2):
            fetch(v, h).start()

    @pl.loop(0, 4)
    def _(v):
        for h in range(2):
            fetch(v, h).wait()
        for c in range(8):
            far = jnp.bitwise_and(yl - c // 2 + NY, NY - 1)
            both = own_ref[jnp.bitwise_xor(core, c % 2), far, v].astype(F32).T.astype(BF16)
            for h in range(2):
                left = both[h * T:(h + 1) * T]
                for s in range(a_ref.shape[3]):
                    b_ref[h, v, c, s] = jnp.dot(left, a_here[v, h, c, s], preferred_element_type=F32).astype(BF16)


def left_products(info, own, a_tiles):
    rows, slots = a_tiles.shape[:2]
    a = a_tiles.reshape(2, 4, 8, slots, T, T)
    vmem = pl.BlockSpec(memory_space=pltpu.VMEM)
    b, done = pl.pallas_call(
        left_kernel,
        in_specs=[pl.BlockSpec(memory_space=pltpu.SMEM), vmem, pl.BlockSpec(memory_space=pltpu.HBM)],
        out_specs=[vmem, vmem],
        out_shape=[jax.ShapeDtypeStruct(a.shape, BF16), jax.ShapeDtypeStruct((8, 2 * T), F32)],
        scratch_shapes=[pltpu.VMEM((4, 2, 8, slots, T, T), BF16), pltpu.SemaphoreType.DMA((4, 2))],
        compiler_params=pltpu.CompilerParams(vmem_limit_bytes=46 * MIB),
        cost_estimate=pl.CostEstimate(flops=2 * rows * slots * T**3, bytes_accessed=16 * MIB, transcendentals=0),
        name="left_products",
    )(info, own, a)
    return b.reshape(rows * slots, T, T), done


def sum_kernel(group, n_chunks, n_before, *refs):
    code_ref, info_ref = refs[:2]
    chunks = refs[2:2 + n_chunks]
    b_ref = refs[2 + n_chunks]
    before = refs[3 + n_chunks:3 + n_chunks + n_before]
    out_ref, panel, acc, sems = refs[-4:]
    core = info_ref[6]
    copies, at = [], 0
    for n, chunk in enumerate(chunks):
        size = chunk.shape[0]
        copies.append(pltpu.make_async_copy(chunk, panel.at[pl.ds(at, size)], sems.at[n]))
        at += size
    for copy in copies:
        copy.start()

    @pl.loop(0, acc.shape[0])
    def _(d):
        acc[d] = jnp.zeros((T, 2 * T), F32)

    for copy in copies:
        copy.wait()
    first = info_ref[group]
    low = lax.broadcasted_iota(I32, (T, 2 * T), 1) < T

    def placed(code):
        pairs = panel[jnp.bitwise_and(jnp.right_shift(code, 9), 127)].astype(F32)
        swap = jnp.bitwise_and(jnp.right_shift(code, 16), 1) == 1
        to_low = jnp.bitwise_and(jnp.right_shift(code, 17), 1) == 0
        pairs = jnp.where(swap, pltpu.roll(pairs, T, 1), pairs)
        return jnp.where(low == to_low, pairs, 0.0).astype(BF16)

    @pl.loop(0, info_ref[3 + group])
    def _(step):
        for half in range(2):
            base = first + step * UNROLL + half * (UNROLL // 2)
            codes = [code_ref[base + e] for e in range(UNROLL // 2)]
            terms = [
                jnp.dot(b_ref[jnp.bitwise_and(code, 511)], placed(code), preferred_element_type=F32)
                for code in codes
            ]
            for code, term in zip(codes, terms):
                d = jnp.right_shift(code, 18)
                acc[d] = acc[d] + term

    @pl.loop(0, KC)
    def _(k):
        for o in range(8):
            tile = jnp.concatenate([acc[k, o * 8:(o + 1) * 8], acc[KC + k, o * 8:(o + 1) * 8]], axis=0)
            place = (jnp.bitwise_xor(core, o % 2), o // 2, k)
            for earlier in before:
                tile = tile + earlier[place].astype(F32)
            out_ref[place] = tile.astype(BF16)


def panel_sums(group, code, info, chunks, b, before=()):
    smem = pl.BlockSpec(memory_space=pltpu.SMEM)
    vmem = pl.BlockSpec(memory_space=pltpu.VMEM)
    anyw = pl.BlockSpec(memory_space=pl.ANY)
    pairs = sum(c.shape[0] for c in chunks)
    return pl.pallas_call(
        functools.partial(sum_kernel, group, len(chunks), len(before)),
        in_specs=[smem, smem] + [anyw] * len(chunks) + [vmem] * (1 + len(before)),
        out_specs=vmem,
        out_shape=jax.ShapeDtypeStruct((2, NY, KC, 16, 2 * T), BF16),
        scratch_shapes=[
            pltpu.VMEM((pairs, T, 2 * T), BF16),
            pltpu.VMEM((2 * KC + 1, T, 2 * T), F32),
            pltpu.SemaphoreType.DMA((len(chunks),)),
        ],
        compiler_params=pltpu.CompilerParams(vmem_limit_bytes=24 * MIB),
        cost_estimate=pl.CostEstimate(flops=pairs * 2**20, bytes_accessed=8 * MIB, transcendentals=0),
        name=f"panel_sums_{group}",
    )(code, info, *chunks, b, *before)


def body(a_tiles, a_cols, a_count, a_slot, agg, p_tiles):
    rows, slots = a_tiles.shape[:2]
    total = rows * slots
    core, yl, me_x = lax.axis_index("core"), lax.axis_index("yl"), lax.axis_index("x")
    me_yh = lax.axis_index("yh")
    packed = jnp.concatenate([p_tiles[0, :4], p_tiles[0, 4:]], axis=-1)

    across = shifted(packed, "yh", 1)
    own = jnp.stack([packed] + [shifted(packed, "yl", k) for k in range(1, NY)])
    near = spread(packed, "z").reshape(-1, T, 2 * T)
    across, near = lax.optimization_barrier((across, near))
    left_a, right_a = shifted(near, "x", 1), shifted(near, "x", -1)
    own = jnp.stack([own, shifted(own, "core", 1)])
    other = spread(across, "z").reshape(-1, T, 2 * T)

    live = jnp.arange(slots, dtype=I32)[None, :] < a_count
    owner = a_cols // 8
    far = jnp.bitwise_and(owner - me_x + 4, 3)
    away = jnp.bitwise_xor((owner // 4) % 2, me_yh)
    group = jnp.where(far == 2, 1 + away, away)
    pair = owner // 8 * 4 + a_cols % 4 + jnp.where(far == 3, 32, jnp.where(far == 1, 64, jnp.where(far == 2, 96 * (1 - away), 0)))
    to_high = jnp.broadcast_to(agg[:, None] % CR, a_cols.shape)
    target = agg[:, None] // CR * KC + a_slot
    swap = ((a_cols % 8) // 4 + to_high) % 2
    code = ((target * 2 + to_high) * 2 + swap) * 2**16 + pair * 2**9 + jnp.arange(total, dtype=I32).reshape(rows, slots)
    code = code.reshape(total)
    picked = (group.reshape(total)[:, None] == jnp.arange(3, dtype=I32)) & live.reshape(total)[:, None]
    lower = jnp.arange(total, dtype=I32)[:, None] > jnp.arange(total, dtype=I32)[None, :]
    rank = jnp.dot(lower.astype(BF16), picked.astype(BF16), preferred_element_type=F32).astype(I32)
    steps = (jnp.sum(picked.astype(I32), axis=0) + UNROLL - 1) // UNROLL
    first = (jnp.cumsum(steps) - steps) * UNROLL
    place = jnp.sum(jnp.where(picked, rank + first[None, :] + 1, 0), axis=1) - 1
    here = jnp.arange(total + 3 * UNROLL, dtype=I32)[:, None] == place[None, :]
    empty = 2 * KC * 2**18
    code = jnp.sum(jnp.where(here, code[None, :] - empty, 0), axis=1) + empty
    info = jnp.concatenate([first, steps, jnp.stack([core, yl])]).astype(I32)

    b, done = left_products(info, own, a_tiles)
    other, _ = lax.optimization_barrier((other, done))
    left_b, right_b = shifted(other, "x", 1), shifted(other, "x", -1)
    left2, right2 = shifted(left_a, "x", 1), shifted(right_b, "x", -1)
    sums0 = panel_sums(0, code, info, [near, left_a, right_a], b)
    sums1 = panel_sums(1, code, info, [other, left_b, right_b, left2], b)
    sums2 = panel_sums(2, code, info, [right2], b, (sums0, sums1))

    chip = (sums2[0].astype(F32) + shifted(sums2[1], "core", 1).astype(F32)).astype(BF16)
    shares = jnp.sum(lax.all_to_all(chip, "yl", 0, 0, tiled=True).astype(F32), axis=0)
    moved = shifted(shares[:, 8:].astype(BF16), ROW, 1)
    result = shares[:, :8] + moved.astype(F32)
    return jnp.stack([result[..., :T], result[..., T:]])


def solution(mesh):
    fine = Mesh(mesh.devices.reshape(8, 2, 4, 4, 2), ROW + COL)
    return jax.shard_map(
        body,
        mesh=fine,
        in_specs=(
            P(ROW, COL, None, None),
            P(ROW, COL),
            P(ROW, COL),
            P(ROW, COL),
            P(ROW),
            P(COL, ROW, None, None),
        ),
        out_specs=P(ROW, None, COL, None),
        check_vma=False,
    )
```

```python
import functools

import jax
import jax.numpy as jnp
from jax import lax
from jax.experimental import pallas as pl
from jax.experimental.pallas import tpu as pltpu
from jax.sharding import Mesh, PartitionSpec as P

KC = 27
CR = 2
T = 64
NY = 4
ROW = ("z", "yh", "x")
COL = ("yl", "core")
UNROLL = 8
F32 = jnp.float32
BF16 = jnp.bfloat16
I32 = jnp.int32
MIB = 2**20


def shifted(value, axis, by):
    count = lax.axis_size(axis)
    return lax.ppermute(value, axis, [(i, (i + by) % count) for i in range(count)])


def spread(value, axis):
    count = lax.axis_size(axis)
    copies = jnp.broadcast_to(value[None], (count,) + value.shape)
    return lax.all_to_all(copies, axis, 0, 0, tiled=True)


def left_kernel(info_ref, own_ref, a_ref, b_ref, done_ref, a_here, sems):
    core, yl = info_ref[6], info_ref[7]
    done_ref[...] = jnp.zeros(done_ref.shape, I32)

    def fetch(v, h):
        return pltpu.make_async_copy(a_ref.at[h, v], a_here.at[v, h], sems.at[v, h])

    for v in range(4):
        for h in range(2):
            fetch(v, h).start()

    @pl.loop(0, 4)
    def _(v):
        for h in range(2):
            fetch(v, h).wait()
        for c in range(8):
            far = jnp.bitwise_and(yl - c // 2 + NY, NY - 1)
            both = own_ref[jnp.bitwise_xor(core, c % 2), far, v].astype(F32).T.astype(BF16)
            for h in range(2):
                left = both[h * T:(h + 1) * T]
                for s in range(a_ref.shape[3]):
                    b_ref[h, v, c, s] = jnp.dot(left, a_here[v, h, c, s], preferred_element_type=F32).astype(BF16)


def left_products(info, own, a_tiles):
    rows, slots = a_tiles.shape[:2]
    a = a_tiles.reshape(2, 4, 8, slots, T, T)
    vmem = pl.BlockSpec(memory_space=pltpu.VMEM)
    b, done = pl.pallas_call(
        left_kernel,
        in_specs=[pl.BlockSpec(memory_space=pltpu.SMEM), vmem, pl.BlockSpec(memory_space=pltpu.HBM)],
        out_specs=[vmem, vmem],
        out_shape=[jax.ShapeDtypeStruct(a.shape, BF16), jax.ShapeDtypeStruct((8, 2 * T), I32)],
        scratch_shapes=[pltpu.VMEM((4, 2, 8, slots, T, T), BF16), pltpu.SemaphoreType.DMA((4, 2))],
        compiler_params=pltpu.CompilerParams(vmem_limit_bytes=48 * MIB),
        cost_estimate=pl.CostEstimate(flops=2 * rows * slots * T**3, bytes_accessed=16 * MIB, transcendentals=0),
        name="left_products",
    )(info, own, a)
    return b.reshape(rows * slots, T, T), done


def sum_kernel(group, n_chunks, n_before, *refs):
    code_ref, info_ref = refs[:2]
    chunks = refs[2:2 + n_chunks]
    b_ref = refs[2 + n_chunks]
    before = refs[3 + n_chunks:3 + n_chunks + n_before]
    out_ref, panel, acc, sems = refs[-4:]
    core = info_ref[6]
    copies, at = [], 0
    for n, chunk in enumerate(chunks):
        size = chunk.shape[0]
        copies.append(pltpu.make_async_copy(chunk, panel.at[pl.ds(at, size)], sems.at[n]))
        at += size
    for copy in copies:
        copy.start()

    @pl.loop(0, acc.shape[0])
    def _(d):
        acc[d] = jnp.zeros((T, 2 * T), F32)

    for copy in copies:
        copy.wait()
    first = info_ref[group]
    low = lax.broadcasted_iota(I32, (T, 2 * T), 1) < T

    def placed(code):
        pairs = panel[jnp.bitwise_and(jnp.right_shift(code, 9), 127)].astype(F32)
        swap = jnp.bitwise_and(jnp.right_shift(code, 16), 1) == 1
        to_low = jnp.bitwise_and(jnp.right_shift(code, 17), 1) == 0
        pairs = jnp.where(swap, pltpu.roll(pairs, T, 1), pairs)
        return jnp.where(low == to_low, pairs, 0.0).astype(BF16)

    @pl.loop(0, info_ref[3 + group])
    def _(step):
        for half in range(2):
            base = first + step * UNROLL + half * (UNROLL // 2)
            codes = [code_ref[base + e] for e in range(UNROLL // 2)]
            terms = [
                jnp.dot(b_ref[jnp.bitwise_and(code, 511)], placed(code), preferred_element_type=F32)
                for code in codes
            ]
            for code, term in zip(codes, terms):
                d = jnp.right_shift(code, 18)
                acc[d] = acc[d] + term

    @pl.loop(0, KC)
    def _(k):
        for o in range(8):
            tile = jnp.concatenate([acc[k, o * 8:(o + 1) * 8], acc[KC + k, o * 8:(o + 1) * 8]], axis=0)
            place = (jnp.bitwise_xor(core, o % 2), o // 2, k)
            for earlier in before:
                tile = tile + earlier[place].astype(F32)
            out_ref[place] = tile.astype(BF16)


def panel_sums(group, code, info, chunks, b, before=()):
    smem = pl.BlockSpec(memory_space=pltpu.SMEM)
    vmem = pl.BlockSpec(memory_space=pltpu.VMEM)
    anyw = pl.BlockSpec(memory_space=pl.ANY)
    pairs = sum(c.shape[0] for c in chunks)
    return pl.pallas_call(
        functools.partial(sum_kernel, group, len(chunks), len(before)),
        in_specs=[smem, smem] + [anyw] * len(chunks) + [vmem] * (1 + len(before)),
        out_specs=vmem,
        out_shape=jax.ShapeDtypeStruct((2, NY, KC, 16, 2 * T), BF16),
        scratch_shapes=[
            pltpu.VMEM((pairs, T, 2 * T), BF16),
            pltpu.VMEM((2 * KC + 1, T, 2 * T), F32),
            pltpu.SemaphoreType.DMA((len(chunks),)),
        ],
        compiler_params=pltpu.CompilerParams(vmem_limit_bytes=14 * MIB),
        cost_estimate=pl.CostEstimate(flops=pairs * 2**20, bytes_accessed=8 * MIB, transcendentals=0),
        name=f"panel_sums_{group}",
    )(code, info, *chunks, b, *before)


def body(a_tiles, a_cols, a_count, a_slot, agg, p_tiles):
    rows, slots = a_tiles.shape[:2]
    total = rows * slots
    core, yl, me_x = lax.axis_index("core"), lax.axis_index("yl"), lax.axis_index("x")
    me_yh = lax.axis_index("yh")
    packed = jnp.concatenate([p_tiles[0, :4], p_tiles[0, 4:]], axis=-1)

    across = shifted(packed, "yh", 1)
    own = jnp.stack([packed] + [shifted(packed, "yl", k) for k in range(1, NY)])
    near = spread(packed, "z").reshape(-1, T, 2 * T)
    across, near = lax.optimization_barrier((across, near))
    left_a, right_a = shifted(near, "x", 1), shifted(near, "x", -1)
    own = jnp.stack([own, shifted(own, "core", 1)])
    other = spread(across, "z").reshape(-1, T, 2 * T)

    live = jnp.arange(slots, dtype=I32)[None, :] < a_count
    owner = a_cols // 8
    far = jnp.bitwise_and(owner - me_x + 4, 3)
    away = jnp.bitwise_xor((owner // 4) % 2, me_yh)
    group = jnp.where(far == 2, 1 + away, away)
    pair = owner // 8 * 4 + a_cols % 4 + jnp.where(far == 3, 32, jnp.where(far == 1, 64, jnp.where(far == 2, 96 * (1 - away), 0)))
    to_high = jnp.broadcast_to(agg[:, None] % CR, a_cols.shape)
    target = agg[:, None] // CR * KC + a_slot
    swap = ((a_cols % 8) // 4 + to_high) % 2
    code = ((target * 2 + to_high) * 2 + swap) * 2**16 + pair * 2**9 + jnp.arange(total, dtype=I32).reshape(rows, slots)
    code = code.reshape(total)
    picked = (group.reshape(total)[:, None] == jnp.arange(3, dtype=I32)) & live.reshape(total)[:, None]
    lower = jnp.arange(total, dtype=I32)[:, None] > jnp.arange(total, dtype=I32)[None, :]
    rank = jnp.dot(lower.astype(BF16), picked.astype(BF16), preferred_element_type=F32).astype(I32)
    steps = (jnp.sum(picked.astype(I32), axis=0) + UNROLL - 1) // UNROLL
    first = (jnp.cumsum(steps) - steps) * UNROLL
    place = jnp.sum(jnp.where(picked, rank + first[None, :] + 1, 0), axis=1) - 1
    here = jnp.arange(total + 3 * UNROLL, dtype=I32)[:, None] == place[None, :]
    empty = 2 * KC * 2**18
    code = jnp.sum(jnp.where(here, code[None, :] - empty, 0), axis=1) + empty
    info = jnp.concatenate([first, steps, jnp.stack([core, yl])]).astype(I32)

    b, done = left_products(info, own, a_tiles)
    other, left_a, right_a, done = lax.optimization_barrier((other, left_a, right_a, done))
    info = info + done[0, :info.shape[0]]
    left_b, right_b = shifted(other, "x", 1), shifted(other, "x", -1)
    left2, right2 = shifted(left_a, "x", 1), shifted(right_b, "x", -1)
    sums0 = panel_sums(0, code, info, [near, left_a, right_a], b)
    sums1 = panel_sums(1, code, info, [other, left_b, right_b, left2], b)
    sums2 = panel_sums(2, code, info, [right2], b, (sums0, sums1))

    chip = (sums2[0].astype(F32) + shifted(sums2[1], "core", 1).astype(F32)).astype(BF16)
    shares = jnp.sum(lax.all_to_all(chip, "yl", 0, 0, tiled=True).astype(F32), axis=0)
    moved = shifted(shares[:, 8:].astype(BF16), ROW, 1)
    result = shares[:, :8] + moved.astype(F32)
    return jnp.stack([result[..., :T], result[..., T:]])


def solution(mesh):
    fine = Mesh(mesh.devices.reshape(8, 2, 4, 4, 2), ROW + COL)
    return jax.shard_map(
        body,
        mesh=fine,
        in_specs=(
            P(ROW, COL, None, None),
            P(ROW, COL),
            P(ROW, COL),
            P(ROW, COL),
            P(ROW),
            P(COL, ROW, None, None),
        ),
        out_specs=P(ROW, None, COL, None),
        check_vma=False,
    )
```

```python
import functools

import jax
import jax.numpy as jnp
from jax import lax
from jax.experimental import pallas as pl
from jax.experimental.pallas import tpu as pltpu
from jax.sharding import Mesh, PartitionSpec as P

KC = 27
CR = 2
T = 64
NY = 4
ROW = ("z", "yh", "x")
COL = ("yl", "core")
UNROLL = 8
F32 = jnp.float32
BF16 = jnp.bfloat16
I32 = jnp.int32
MIB = 2**20


def shifted(value, axis, by):
    count = lax.axis_size(axis)
    return lax.ppermute(value, axis, [(i, (i + by) % count) for i in range(count)])


def swapped(value, axis, by):
    return lax.ppermute(value, axis, [(i, i ^ by) for i in range(lax.axis_size(axis))])


def spread(value, axis):
    count = lax.axis_size(axis)
    copies = jnp.broadcast_to(value[None], (count,) + value.shape)
    return lax.all_to_all(copies, axis, 0, 0, tiled=True)


def left_kernel(info_ref, own_ref, a_ref, b_ref, a_here, sems):
    core, yl = info_ref[6], info_ref[7]

    def fetch(v, h):
        return pltpu.make_async_copy(a_ref.at[h, v], a_here.at[v, h], sems.at[v, h])

    for v in range(4):
        for h in range(2):
            fetch(v, h).start()

    @pl.loop(0, 4)
    def _(v):
        for h in range(2):
            fetch(v, h).wait()
        for c in range(8):
            far = jnp.bitwise_xor(yl, c // 2)
            both = own_ref[jnp.bitwise_xor(core, c % 2), far, v].astype(F32).T.astype(BF16)
            for h in range(2):
                left = both[h * T:(h + 1) * T]
                for s in range(a_ref.shape[3]):
                    b_ref[h, v, c, s] = jnp.dot(left, a_here[v, h, c, s], preferred_element_type=F32).astype(BF16)


def left_products(info, own, a_tiles):
    rows, slots = a_tiles.shape[:2]
    a = a_tiles.reshape(2, 4, 8, slots, T, T)
    vmem = pl.BlockSpec(memory_space=pltpu.VMEM)
    b = pl.pallas_call(
        left_kernel,
        in_specs=[pl.BlockSpec(memory_space=pltpu.SMEM), vmem, pl.BlockSpec(memory_space=pltpu.HBM)],
        out_specs=vmem,
        out_shape=jax.ShapeDtypeStruct(a.shape, BF16),
        scratch_shapes=[pltpu.VMEM((4, 2, 8, slots, T, T), BF16), pltpu.SemaphoreType.DMA((4, 2))],
        compiler_params=pltpu.CompilerParams(vmem_limit_bytes=46 * MIB),
        cost_estimate=pl.CostEstimate(flops=2 * rows * slots * T**3, bytes_accessed=16 * MIB, transcendentals=0),
        name="left_products",
    )(info, own, a)
    return b.reshape(rows * slots, T, T)


def sum_kernel(group, n_chunks, n_before, *refs):
    code_ref, info_ref = refs[:2]
    chunks = refs[2:2 + n_chunks]
    b_ref = refs[2 + n_chunks]
    before = refs[3 + n_chunks:3 + n_chunks + n_before]
    out_ref, panel, acc, sems = refs[-4:]
    core, yl = info_ref[6], info_ref[7]
    copies, at = [], 0
    for n, chunk in enumerate(chunks):
        size = chunk.shape[0]
        copies.append(pltpu.make_async_copy(chunk, panel.at[pl.ds(at, size)], sems.at[n]))
        at += size
    for copy in copies:
        copy.start()

    @pl.loop(0, acc.shape[0])
    def _(d):
        acc[d] = jnp.zeros((T, 2 * T), F32)

    for copy in copies:
        copy.wait()
    first = info_ref[group]
    low = lax.broadcasted_iota(I32, (T, 2 * T), 1) < T

    def placed(code):
        pairs = panel[jnp.bitwise_and(jnp.right_shift(code, 9), 127)].astype(F32)
        swap = jnp.bitwise_and(jnp.right_shift(code, 16), 1) == 1
        to_low = jnp.bitwise_and(jnp.right_shift(code, 17), 1) == 0
        pairs = jnp.where(swap, pltpu.roll(pairs, T, 1), pairs)
        return jnp.where(low == to_low, pairs, 0.0).astype(BF16)

    @pl.loop(0, info_ref[3 + group])
    def _(step):
        for half in range(2):
            base = first + step * UNROLL + half * (UNROLL // 2)
            codes = [code_ref[base + e] for e in range(UNROLL // 2)]
            terms = [
                jnp.dot(b_ref[jnp.bitwise_and(code, 511)], placed(code), preferred_element_type=F32)
                for code in codes
            ]
            for code, term in zip(codes, terms):
                d = jnp.right_shift(code, 18)
                acc[d] = acc[d] + term

    @pl.loop(0, KC)
    def _(k):
        for o in range(8):
            tile = jnp.concatenate([acc[k, o * 8:(o + 1) * 8], acc[KC + k, o * 8:(o + 1) * 8]], axis=0)
            far = jnp.bitwise_xor(yl, o // 2)
            place = (jnp.bitwise_xor(core, o % 2), jnp.bitwise_and(far, 1), jnp.right_shift(far, 1), k)
            for earlier in before:
                tile = tile + earlier[place].astype(F32)
            out_ref[place] = tile.astype(BF16)


def panel_sums(group, code, info, chunks, b, before=()):
    smem = pl.BlockSpec(memory_space=pltpu.SMEM)
    vmem = pl.BlockSpec(memory_space=pltpu.VMEM)
    anyw = pl.BlockSpec(memory_space=pl.ANY)
    pairs = sum(c.shape[0] for c in chunks)
    return pl.pallas_call(
        functools.partial(sum_kernel, group, len(chunks), len(before)),
        in_specs=[smem, smem] + [anyw] * len(chunks) + [vmem] * (1 + len(before)),
        out_specs=vmem,
        out_shape=jax.ShapeDtypeStruct((2, 2, 2, KC, 16, 2 * T), BF16),
        scratch_shapes=[
            pltpu.VMEM((pairs, T, 2 * T), BF16),
            pltpu.VMEM((2 * KC + 1, T, 2 * T), F32),
            pltpu.SemaphoreType.DMA((len(chunks),)),
        ],
        compiler_params=pltpu.CompilerParams(vmem_limit_bytes=24 * MIB),
        cost_estimate=pl.CostEstimate(flops=pairs * 2**20, bytes_accessed=8 * MIB, transcendentals=0),
        name=f"panel_sums_{group}",
    )(code, info, *chunks, b, *before)


def body(a_tiles, a_cols, a_count, a_slot, agg, p_tiles):
    rows, slots = a_tiles.shape[:2]
    total = rows * slots
    core, yl, me_x = lax.axis_index("core"), lax.axis_index("yl"), lax.axis_index("x")
    me_yh = lax.axis_index("yh")
    packed = jnp.concatenate([p_tiles[0, :4], p_tiles[0, 4:]], axis=-1)

    across = shifted(packed, "yh", 1)
    near = spread(packed, "z").reshape(-1, T, 2 * T)
    across, near, packed = lax.optimization_barrier((across, near, packed))
    left_a, right_a = shifted(near, "x", 1), shifted(near, "x", -1)
    other = spread(across, "z").reshape(-1, T, 2 * T)
    own = jnp.stack([packed, swapped(packed, "yl", 1)])
    own = jnp.concatenate([own, swapped(own, "yl", 2)])
    own = jnp.stack([own, swapped(own, "core", 1)])

    live = jnp.arange(slots, dtype=I32)[None, :] < a_count
    owner = a_cols // 8
    far = jnp.bitwise_and(owner - me_x + 4, 3)
    away = jnp.bitwise_xor((owner // 4) % 2, me_yh)
    group = jnp.where(far == 2, 1 + away, away)
    pair = owner // 8 * 4 + a_cols % 4 + jnp.where(far == 3, 32, jnp.where(far == 1, 64, jnp.where(far == 2, 96 * (1 - away), 0)))
    to_high = jnp.broadcast_to(agg[:, None] % CR, a_cols.shape)
    target = agg[:, None] // CR * KC + a_slot
    swap = ((a_cols % 8) // 4 + to_high) % 2
    code = ((target * 2 + to_high) * 2 + swap) * 2**16 + pair * 2**9 + jnp.arange(total, dtype=I32).reshape(rows, slots)
    code = code.reshape(total)
    picked = (group.reshape(total)[:, None] == jnp.arange(3, dtype=I32)) & live.reshape(total)[:, None]
    lower = jnp.arange(total, dtype=I32)[:, None] > jnp.arange(total, dtype=I32)[None, :]
    rank = jnp.dot(lower.astype(BF16), picked.astype(BF16), preferred_element_type=F32).astype(I32)
    steps = (jnp.sum(picked.astype(I32), axis=0) + UNROLL - 1) // UNROLL
    first = (jnp.cumsum(steps) - steps) * UNROLL
    place = jnp.sum(jnp.where(picked, rank + first[None, :] + 1, 0), axis=1) - 1
    here = jnp.arange(total + 3 * UNROLL, dtype=I32)[:, None] == place[None, :]
    empty = 2 * KC * 2**18
    code = jnp.sum(jnp.where(here, code[None, :] - empty, 0), axis=1) + empty
    info = jnp.concatenate([first, steps, jnp.stack([core, yl])]).astype(I32)

    other, left_a, right_a, own, info, code = lax.optimization_barrier((other, left_a, right_a, own, info, code))
    left_b, right_b = shifted(other, "x", 1), shifted(other, "x", -1)
    left2, right2 = shifted(left_a, "x", 1), shifted(right_b, "x", -1)
    b = left_products(info, own, a_tiles)
    sums0 = panel_sums(0, code, info, [near, left_a, right_a], b)
    sums1 = panel_sums(1, code, info, [other, left_b, right_b, left2], b)
    sums2 = panel_sums(2, code, info, [right2], b, (sums0, sums1))

    chip = (sums2[0].astype(F32) + swapped(sums2[1], "core", 1).astype(F32)).astype(BF16)
    two = chip[0].astype(F32) + swapped(chip[1], "yl", 1).astype(F32)
    mine, theirs = two[0], two[1].astype(BF16)
    count = lax.axis_size(ROW)
    ahead = [[(r * NY + y, (r + 1) % count * NY + (y ^ by)) for r in range(count) for y in range(NY)] for by in (0, 2)]
    last = [
        lax.ppermute(theirs[:, 8:], ROW + ("yl",), ahead[1]),
        lax.ppermute(mine[:, 8:].astype(BF16), ROW + ("yl",), ahead[0]),
        swapped(theirs[:, :8], "yl", 2),
    ]
    result = mine[:, :8] + sum(part.astype(F32) for part in last)
    return jnp.stack([result[..., :T], result[..., T:]])


def solution(mesh):
    fine = Mesh(mesh.devices.reshape(8, 2, 4, 4, 2), ROW + COL)
    return jax.shard_map(
        body,
        mesh=fine,
        in_specs=(
            P(ROW, COL, None, None),
            P(ROW, COL),
            P(ROW, COL),
            P(ROW, COL),
            P(ROW),
            P(COL, ROW, None, None),
        ),
        out_specs=P(ROW, None, COL, None),
        check_vma=False,
    )
```

```python
import functools

import jax
import jax.numpy as jnp
from jax import lax
from jax.experimental import pallas as pl
from jax.experimental.pallas import tpu as pltpu
from jax.sharding import Mesh, PartitionSpec as P

KC = 27
CR = 2
T = 64
NY = 4
ROW = ("z", "yh", "x")
COL = ("yl", "core")
UNROLL = 8
F32 = jnp.float32
BF16 = jnp.bfloat16
I32 = jnp.int32
MIB = 2**20


def shifted(value, axis, by):
    count = lax.axis_size(axis)
    return lax.ppermute(value, axis, [(i, (i + by) % count) for i in range(count)])


def swapped(value, axis, by):
    return lax.ppermute(value, axis, [(i, i ^ by) for i in range(lax.axis_size(axis))])


def spread(value, axis):
    count = lax.axis_size(axis)
    copies = jnp.broadcast_to(value[None], (count,) + value.shape)
    return lax.all_to_all(copies, axis, 0, 0, tiled=True)


def left_kernel(own_ref, a_ref, b_ref, a_here, sems):
    def fetch(v, h):
        return pltpu.make_async_copy(a_ref.at[h, v], a_here.at[v, h], sems.at[v, h])

    for v in range(4):
        for h in range(2):
            fetch(v, h).start()

    @pl.loop(0, 4)
    def _(v):
        for h in range(2):
            fetch(v, h).wait()
        for c in range(8):
            both = own_ref[c, v].astype(F32).T.astype(BF16)
            for h in range(2):
                left = both[h * T:(h + 1) * T]
                for s in range(a_ref.shape[3]):
                    b_ref[h, v, c, s] = jnp.dot(left, a_here[v, h, c, s], preferred_element_type=F32).astype(BF16)


def left_products(own, a_tiles):
    rows, slots = a_tiles.shape[:2]
    a = a_tiles.reshape(2, 4, 8, slots, T, T)
    vmem = pl.BlockSpec(memory_space=pltpu.VMEM)
    b = pl.pallas_call(
        left_kernel,
        in_specs=[vmem, pl.BlockSpec(memory_space=pltpu.HBM)],
        out_specs=vmem,
        out_shape=jax.ShapeDtypeStruct(a.shape, BF16),
        scratch_shapes=[pltpu.VMEM((4, 2, 8, slots, T, T), BF16), pltpu.SemaphoreType.DMA((4, 2))],
        compiler_params=pltpu.CompilerParams(vmem_limit_bytes=46 * MIB),
        cost_estimate=pl.CostEstimate(flops=2 * rows * slots * T**3, bytes_accessed=16 * MIB, transcendentals=0),
        name="left_products",
    )(own, a)
    return b.reshape(rows * slots, T, T)


def sum_kernel(group, n_chunks, n_before, *refs):
    code_ref, info_ref = refs[:2]
    chunks = refs[2:2 + n_chunks]
    b_ref = refs[2 + n_chunks]
    before = refs[3 + n_chunks:3 + n_chunks + n_before]
    out_ref, panel, acc, sems = refs[-4:]
    core, yl = info_ref[6], info_ref[7]
    copies, at = [], 0
    for n, chunk in enumerate(chunks):
        size = chunk.shape[0]
        copies.append(pltpu.make_async_copy(chunk, panel.at[pl.ds(at, size)], sems.at[n]))
        at += size
    for copy in copies:
        copy.start()

    @pl.loop(0, acc.shape[0])
    def _(d):
        acc[d] = jnp.zeros((T, 2 * T), F32)

    for copy in copies:
        copy.wait()
    first = info_ref[group]
    low = lax.broadcasted_iota(I32, (T, 2 * T), 1) < T

    def placed(code):
        pairs = panel[jnp.bitwise_and(jnp.right_shift(code, 9), 127)].astype(F32)
        swap = jnp.bitwise_and(jnp.right_shift(code, 16), 1) == 1
        to_low = jnp.bitwise_and(jnp.right_shift(code, 17), 1) == 0
        pairs = jnp.where(swap, pltpu.roll(pairs, T, 1), pairs)
        return jnp.where(low == to_low, pairs, 0.0).astype(BF16)

    @pl.loop(0, info_ref[3 + group])
    def _(step):
        for half in range(2):
            base = first + step * UNROLL + half * (UNROLL // 2)
            codes = [code_ref[base + e] for e in range(UNROLL // 2)]
            terms = [
                jnp.dot(b_ref[jnp.bitwise_and(code, 511)], placed(code), preferred_element_type=F32)
                for code in codes
            ]
            for code, term in zip(codes, terms):
                d = jnp.right_shift(code, 18)
                acc[d] = acc[d] + term

    @pl.loop(0, KC)
    def _(k):
        for o in range(8):
            tile = jnp.concatenate([acc[k, o * 8:(o + 1) * 8], acc[KC + k, o * 8:(o + 1) * 8]], axis=0)
            far = jnp.bitwise_xor(yl, o // 2)
            place = (jnp.bitwise_xor(core, o % 2), jnp.bitwise_and(far, 1), jnp.right_shift(far, 1), k)
            for earlier in before:
                tile = tile + earlier[place].astype(F32)
            out_ref[place] = tile.astype(BF16)


def panel_sums(group, code, info, chunks, b, before=()):
    smem = pl.BlockSpec(memory_space=pltpu.SMEM)
    vmem = pl.BlockSpec(memory_space=pltpu.VMEM)
    anyw = pl.BlockSpec(memory_space=pl.ANY)
    pairs = sum(c.shape[0] for c in chunks)
    return pl.pallas_call(
        functools.partial(sum_kernel, group, len(chunks), len(before)),
        in_specs=[smem, smem] + [anyw] * len(chunks) + [vmem] * (1 + len(before)),
        out_specs=vmem,
        out_shape=jax.ShapeDtypeStruct((2, 2, 2, KC, 16, 2 * T), BF16),
        scratch_shapes=[
            pltpu.VMEM((pairs, T, 2 * T), BF16),
            pltpu.VMEM((2 * KC + 1, T, 2 * T), F32),
            pltpu.SemaphoreType.DMA((len(chunks),)),
        ],
        compiler_params=pltpu.CompilerParams(vmem_limit_bytes=24 * MIB),
        cost_estimate=pl.CostEstimate(flops=pairs * 2**20, bytes_accessed=8 * MIB, transcendentals=0),
        name=f"panel_sums_{group}",
    )(code, info, *chunks, b, *before)


def body(a_tiles, a_cols, a_count, a_slot, agg, p_tiles):
    rows, slots = a_tiles.shape[:2]
    total = rows * slots
    core, yl, me_x = lax.axis_index("core"), lax.axis_index("yl"), lax.axis_index("x")
    packed = jnp.concatenate([p_tiles[0, :4], p_tiles[0, 4:]], axis=-1)

    live = jnp.arange(slots, dtype=I32)[None, :] < a_count
    owner = a_cols // 8
    far = jnp.bitwise_and(owner - me_x + 4, 3)
    high = (owner // 4) % 2
    group = jnp.where(far == 0, 0, jnp.where(far == 2, 2, jnp.where((far == 3) == (high == 0), 0, 1)))
    seat = jnp.where(far == 1, 3 - 2 * (1 - high), jnp.where(far == 3, 2 * (1 - high), high))
    pair = seat * 32 + owner // 8 * 4 + a_cols % 4
    to_high = jnp.broadcast_to(agg[:, None] % CR, a_cols.shape)
    target = agg[:, None] // CR * KC + a_slot
    swap = ((a_cols % 8) // 4 + to_high) % 2
    code = ((target * 2 + to_high) * 2 + swap) * 2**16 + pair * 2**9 + jnp.arange(total, dtype=I32).reshape(rows, slots)
    code = code.reshape(total)
    picked = (group.reshape(total)[:, None] == jnp.arange(3, dtype=I32)) & live.reshape(total)[:, None]
    lower = jnp.arange(total, dtype=I32)[:, None] > jnp.arange(total, dtype=I32)[None, :]
    rank = jnp.dot(lower.astype(BF16), picked.astype(BF16), preferred_element_type=F32).astype(I32)
    steps = (jnp.sum(picked.astype(I32), axis=0) + UNROLL - 1) // UNROLL
    first = (jnp.cumsum(steps) - steps) * UNROLL
    place = jnp.sum(jnp.where(picked, rank + first[None, :] + 1, 0), axis=1) - 1
    here = jnp.arange(total + 3 * UNROLL, dtype=I32)[:, None] == place[None, :]
    empty = 2 * KC * 2**18
    code = jnp.sum(jnp.where(here, code[None, :] - empty, 0), axis=1) + empty
    info = jnp.concatenate([first, steps, jnp.stack([core, yl])]).astype(I32)

    column = spread(packed, ("yh", "z")).reshape(-1, T, 2 * T)
    column, packed, info, code = lax.optimization_barrier((column, packed, info, code))
    low, high = column[:column.shape[0] // 2], column[column.shape[0] // 2:]
    left_a, right_b = shifted(low, "x", 1), shifted(high, "x", -1)
    left_b, right_a = shifted(high, "x", 1), shifted(low, "x", -1)
    left2, right2 = shifted(left_a, "x", 1), shifted(right_b, "x", -1)

    b = left_products(spread(packed, COL), a_tiles)
    sums0 = panel_sums(0, code, info, [column, left_a, right_b], b)
    sums1 = panel_sums(1, code, info, [left_b, right_a], b)
    sums2 = panel_sums(2, code, info, [left2, right2], b, (sums0, sums1))

    chip = (sums2[0].astype(F32) + swapped(sums2[1], "core", 1).astype(F32)).astype(BF16)
    two = chip[0].astype(F32) + swapped(chip[1], "yl", 1).astype(F32)
    mine, theirs = two[0], two[1].astype(BF16)
    count = lax.axis_size(ROW)
    ahead = [[(r * NY + y, (r + 1) % count * NY + (y ^ by)) for r in range(count) for y in range(NY)] for by in (0, 2)]
    last = [
        swapped(theirs[:, :8], "yl", 2),
        lax.ppermute(mine[:, 8:].astype(BF16), ROW + ("yl",), ahead[0]),
        lax.ppermute(theirs[:, 8:], ROW + ("yl",), ahead[1]),
    ]
    result = mine[:, :8] + sum(part.astype(F32) for part in last)
    return jnp.stack([result[..., :T], result[..., T:]])


def solution(mesh):
    fine = Mesh(mesh.devices.reshape(8, 2, 4, 4, 2), ROW + COL)
    return jax.shard_map(
        body,
        mesh=fine,
        in_specs=(
            P(ROW, COL, None, None),
            P(ROW, COL),
            P(ROW, COL),
            P(ROW, COL),
            P(ROW),
            P(COL, ROW, None, None),
        ),
        out_specs=P(ROW, None, COL, None),
        check_vma=False,
    )
```

```python
import functools

import jax
import jax.numpy as jnp
from jax import lax
from jax.experimental import pallas as pl
from jax.experimental.pallas import tpu as pltpu
from jax.sharding import Mesh, PartitionSpec as P

KC = 27
CR = 2
T = 64
NY = 4
ROW = ("z", "yh", "x")
COL = ("yl", "core")
UNROLL = 8
F32 = jnp.float32
BF16 = jnp.bfloat16
I32 = jnp.int32
MIB = 2**20


def shifted(value, axis, by):
    count = lax.axis_size(axis)
    return lax.ppermute(value, axis, [(i, (i + by) % count) for i in range(count)])


def swapped(value, axis, by):
    return lax.ppermute(value, axis, [(i, i ^ by) for i in range(lax.axis_size(axis))])


def spread(value, axis):
    count = lax.axis_size(axis)
    copies = jnp.broadcast_to(value[None], (count,) + value.shape)
    return lax.all_to_all(copies, axis, 0, 0, tiled=True)


def left_kernel(own_ref, a_ref, b_ref, a_here, sems):
    def fetch(v, h):
        return pltpu.make_async_copy(a_ref.at[h, v], a_here.at[v, h], sems.at[v, h])

    for v in range(4):
        for h in range(2):
            fetch(v, h).start()

    @pl.loop(0, 4)
    def _(v):
        for h in range(2):
            fetch(v, h).wait()
        for c in range(8):
            both = own_ref[c, v].astype(F32).T.astype(BF16)
            for h in range(2):
                left = both[h * T:(h + 1) * T]
                for s in range(a_ref.shape[3]):
                    b_ref[h, v, c, s] = jnp.dot(left, a_here[v, h, c, s], preferred_element_type=F32).astype(BF16)


def left_products(own, a_tiles):
    rows, slots = a_tiles.shape[:2]
    a = a_tiles.reshape(2, 4, 8, slots, T, T)
    vmem = pl.BlockSpec(memory_space=pltpu.VMEM)
    b = pl.pallas_call(
        left_kernel,
        in_specs=[vmem, pl.BlockSpec(memory_space=pltpu.HBM)],
        out_specs=vmem,
        out_shape=jax.ShapeDtypeStruct(a.shape, BF16),
        scratch_shapes=[pltpu.VMEM((4, 2, 8, slots, T, T), BF16), pltpu.SemaphoreType.DMA((4, 2))],
        compiler_params=pltpu.CompilerParams(vmem_limit_bytes=46 * MIB),
        cost_estimate=pl.CostEstimate(flops=2 * rows * slots * T**3, bytes_accessed=16 * MIB, transcendentals=0),
        name="left_products",
    )(own, a)
    return b.reshape(rows * slots, T, T)


def sum_kernel(group, n_chunks, n_before, *refs):
    code_ref, info_ref = refs[:2]
    chunks = refs[2:2 + n_chunks]
    b_ref = refs[2 + n_chunks]
    before = refs[3 + n_chunks:3 + n_chunks + n_before]
    out_ref, panel, acc, sems = refs[-4:]
    core = info_ref[6]
    copies, at = [], 0
    for n, chunk in enumerate(chunks):
        size = chunk.shape[0]
        copies.append(pltpu.make_async_copy(chunk, panel.at[pl.ds(at, size)], sems.at[n]))
        at += size
    for copy in copies:
        copy.start()

    @pl.loop(0, acc.shape[0])
    def _(d):
        acc[d] = jnp.zeros((T, 2 * T), F32)

    for copy in copies:
        copy.wait()
    first = info_ref[group]
    low = lax.broadcasted_iota(I32, (T, 2 * T), 1) < T

    def placed(code):
        pairs = panel[jnp.bitwise_and(jnp.right_shift(code, 9), 127)].astype(F32)
        swap = jnp.bitwise_and(jnp.right_shift(code, 16), 1) == 1
        to_low = jnp.bitwise_and(jnp.right_shift(code, 17), 1) == 0
        pairs = jnp.where(swap, pltpu.roll(pairs, T, 1), pairs)
        return jnp.where(low == to_low, pairs, 0.0).astype(BF16)

    @pl.loop(0, info_ref[3 + group])
    def _(step):
        for half in range(2):
            base = first + step * UNROLL + half * (UNROLL // 2)
            codes = [code_ref[base + e] for e in range(UNROLL // 2)]
            terms = [
                jnp.dot(b_ref[jnp.bitwise_and(code, 511)], placed(code), preferred_element_type=F32)
                for code in codes
            ]
            for code, term in zip(codes, terms):
                d = jnp.right_shift(code, 18)
                acc[d] = acc[d] + term

    @pl.loop(0, KC)
    def _(k):
        for o in range(8):
            tile = jnp.concatenate([acc[k, o * 8:(o + 1) * 8], acc[KC + k, o * 8:(o + 1) * 8]], axis=0)
            place = (jnp.bitwise_xor(core, o % 2), o // 4, o // 2 % 2, k)
            for earlier in before:
                tile = tile + earlier[place].astype(F32)
            out_ref[place] = tile.astype(BF16)


def panel_sums(group, code, info, chunks, b, before=()):
    smem = pl.BlockSpec(memory_space=pltpu.SMEM)
    vmem = pl.BlockSpec(memory_space=pltpu.VMEM)
    anyw = pl.BlockSpec(memory_space=pl.ANY)
    pairs = sum(c.shape[0] for c in chunks)
    return pl.pallas_call(
        functools.partial(sum_kernel, group, len(chunks), len(before)),
        in_specs=[smem, smem] + [anyw] * len(chunks) + [vmem] * (1 + len(before)),
        out_specs=vmem,
        out_shape=jax.ShapeDtypeStruct((2, 2, 2, KC, 16, 2 * T), BF16),
        scratch_shapes=[
            pltpu.VMEM((pairs, T, 2 * T), BF16),
            pltpu.VMEM((2 * KC + 1, T, 2 * T), F32),
            pltpu.SemaphoreType.DMA((len(chunks),)),
        ],
        compiler_params=pltpu.CompilerParams(vmem_limit_bytes=24 * MIB),
        cost_estimate=pl.CostEstimate(flops=pairs * 2**20, bytes_accessed=8 * MIB, transcendentals=0),
        name=f"panel_sums_{group}",
    )(code, info, *chunks, b, *before)


def body(a_tiles, a_cols, a_count, a_slot, agg, p_tiles):
    rows, slots = a_tiles.shape[:2]
    total = rows * slots
    core, yl, me_x = lax.axis_index("core"), lax.axis_index("yl"), lax.axis_index("x")
    packed = jnp.concatenate([p_tiles[0, :4], p_tiles[0, 4:]], axis=-1)

    live = jnp.arange(slots, dtype=I32)[None, :] < a_count
    owner = a_cols // 8
    far = jnp.bitwise_and(owner - me_x + 4, 3)
    high = (owner // 4) % 2
    group = jnp.where(far == 0, 0, jnp.where(far == 2, 2, jnp.where((far == 3) == (high == 0), 0, 1)))
    seat = jnp.where(far == 1, 3 - 2 * (1 - high), jnp.where(far == 3, 2 * (1 - high), high))
    pair = seat * 32 + owner // 8 * 4 + a_cols % 4
    to_high = jnp.broadcast_to(agg[:, None] % CR, a_cols.shape)
    target = agg[:, None] // CR * KC + a_slot
    swap = ((a_cols % 8) // 4 + to_high) % 2
    code = ((target * 2 + to_high) * 2 + swap) * 2**16 + pair * 2**9 + jnp.arange(total, dtype=I32).reshape(rows, slots)
    code = code.reshape(total)
    picked = (group.reshape(total)[:, None] == jnp.arange(3, dtype=I32)) & live.reshape(total)[:, None]
    lower = jnp.arange(total, dtype=I32)[:, None] > jnp.arange(total, dtype=I32)[None, :]
    rank = jnp.dot(lower.astype(BF16), picked.astype(BF16), preferred_element_type=F32).astype(I32)
    steps = (jnp.sum(picked.astype(I32), axis=0) + UNROLL - 1) // UNROLL
    first = (jnp.cumsum(steps) - steps) * UNROLL
    place = jnp.sum(jnp.where(picked, rank + first[None, :] + 1, 0), axis=1) - 1
    here = jnp.arange(total + 3 * UNROLL, dtype=I32)[:, None] == place[None, :]
    empty = 2 * KC * 2**18
    code = jnp.sum(jnp.where(here, code[None, :] - empty, 0), axis=1) + empty
    info = jnp.concatenate([first, steps, jnp.stack([core, yl])]).astype(I32)

    column = spread(packed, ("yh", "z")).reshape(-1, T, 2 * T)
    column, packed, info, code = lax.optimization_barrier((column, packed, info, code))
    low, high = column[:column.shape[0] // 2], column[column.shape[0] // 2:]
    left_a, right_b = shifted(low, "x", 1), shifted(high, "x", -1)
    left_b, right_a = shifted(high, "x", 1), shifted(low, "x", -1)
    left2, right2 = shifted(left_a, "x", 1), shifted(right_b, "x", -1)

    b = left_products(spread(packed, COL), a_tiles)
    sums0 = panel_sums(0, code, info, [column, left_a, right_b], b)
    sums1 = panel_sums(1, code, info, [left_b, right_a], b)
    sums2 = panel_sums(2, code, info, [left2, right2], b, (sums0, sums1))

    chip = sums2[0].astype(F32) + swapped(sums2[1], "core", 1).astype(F32)
    staying = chip[..., :8, :].astype(BF16).reshape(NY, KC, 8, 2 * T)
    staying = lax.all_to_all(staying, "yl", 0, 0, tiled=True)
    coming = chip[..., 8:, :].astype(BF16)
    bit0, bit1 = yl % 2, yl // 2
    pick = functools.partial(lax.dynamic_index_in_dim, keepdims=False)
    two = pick(coming, bit0, 1).astype(F32) + swapped(pick(coming, 1 - bit0, 1), "yl", 1).astype(F32)
    count = lax.axis_size(ROW)
    ahead = [[(r * NY + y, (r + 1) % count * NY + (y ^ by)) for r in range(count) for y in range(NY)] for by in (0, 2)]
    last = [
        lax.ppermute(pick(two, bit1, 0).astype(BF16), ROW + ("yl",), ahead[0]),
        lax.ppermute(pick(two, 1 - bit1, 0).astype(BF16), ROW + ("yl",), ahead[1]),
    ]
    result = jnp.sum(staying.astype(F32), axis=0) + sum(part.astype(F32) for part in last)
    return jnp.stack([result[..., :T], result[..., T:]])


def solution(mesh):
    fine = Mesh(mesh.devices.reshape(8, 2, 4, 4, 2), ROW + COL)
    return jax.shard_map(
        body,
        mesh=fine,
        in_specs=(
            P(ROW, COL, None, None),
            P(ROW, COL),
            P(ROW, COL),
            P(ROW, COL),
            P(ROW),
            P(COL, ROW, None, None),
        ),
        out_specs=P(ROW, None, COL, None),
        check_vma=False,
    )
```

```python
import functools

import jax
import jax.numpy as jnp
from jax import lax
from jax.experimental import pallas as pl
from jax.experimental.pallas import tpu as pltpu
from jax.sharding import Mesh, PartitionSpec as P

KC = 27
KP = 28
CR = 2
T = 64
NY = 4
ROW = ("z", "yh", "x")
COL = ("yl", "core")
UNROLL = 8
F32 = jnp.float32
BF16 = jnp.bfloat16
I32 = jnp.int32
MIB = 2**20


def shifted(value, axis, by):
    count = lax.axis_size(axis)
    return lax.ppermute(value, axis, [(i, (i + by) % count) for i in range(count)])


def swapped(value, axis, by):
    return lax.ppermute(value, axis, [(i, i ^ by) for i in range(lax.axis_size(axis))])


def spread(value, axis):
    count = lax.axis_size(axis)
    copies = jnp.broadcast_to(value[None], (count,) + value.shape)
    return lax.all_to_all(copies, axis, 0, 0, tiled=True)


def left_kernel(own_ref, a_ref, b_ref, a_here, sems):
    def fetch(v, h):
        return pltpu.make_async_copy(a_ref.at[h, v], a_here.at[v, h], sems.at[v, h])

    for v in range(4):
        for h in range(2):
            fetch(v, h).start()

    @pl.loop(0, 4)
    def _(v):
        for h in range(2):
            fetch(v, h).wait()
        for c in range(8):
            both = own_ref[c, v].astype(F32).T.astype(BF16)
            for h in range(2):
                left = both[h * T:(h + 1) * T]
                for s in range(a_ref.shape[3]):
                    b_ref[h, v, c, s] = jnp.dot(left, a_here[v, h, c, s], preferred_element_type=F32).astype(BF16)


def left_products(own, a_tiles):
    rows, slots = a_tiles.shape[:2]
    a = a_tiles.reshape(2, 4, 8, slots, T, T)
    vmem = pl.BlockSpec(memory_space=pltpu.VMEM)
    b = pl.pallas_call(
        left_kernel,
        in_specs=[vmem, pl.BlockSpec(memory_space=pltpu.HBM)],
        out_specs=vmem,
        out_shape=jax.ShapeDtypeStruct(a.shape, BF16),
        scratch_shapes=[pltpu.VMEM((4, 2, 8, slots, T, T), BF16), pltpu.SemaphoreType.DMA((4, 2))],
        compiler_params=pltpu.CompilerParams(vmem_limit_bytes=46 * MIB),
        cost_estimate=pl.CostEstimate(flops=2 * rows * slots * T**3, bytes_accessed=16 * MIB, transcendentals=0),
        name="left_products",
    )(own, a)
    return b.reshape(rows * slots, T, T)


def sum_kernel(group, n_chunks, n_before, *refs):
    code_ref, info_ref = refs[:2]
    chunks = refs[2:2 + n_chunks]
    b_ref = refs[2 + n_chunks]
    before = refs[3 + n_chunks:3 + n_chunks + n_before]
    out_ref, panel, acc, sems = refs[-4:]
    core, yl = info_ref[6], info_ref[7]
    copies, at = [], 0
    for n, chunk in enumerate(chunks):
        size = chunk.shape[0]
        copies.append(pltpu.make_async_copy(chunk, panel.at[pl.ds(at, size)], sems.at[n]))
        at += size
    for copy in copies:
        copy.start()

    @pl.loop(0, acc.shape[0])
    def _(d):
        acc[d] = jnp.zeros((T, 2 * T), F32)

    for copy in copies:
        copy.wait()
    first = info_ref[group]
    low = lax.broadcasted_iota(I32, (T, 2 * T), 1) < T

    def placed(code):
        pairs = panel[jnp.bitwise_and(jnp.right_shift(code, 9), 127)].astype(F32)
        swap = jnp.bitwise_and(jnp.right_shift(code, 16), 1) == 1
        to_low = jnp.bitwise_and(jnp.right_shift(code, 17), 1) == 0
        pairs = jnp.where(swap, pltpu.roll(pairs, T, 1), pairs)
        return jnp.where(low == to_low, pairs, 0.0).astype(BF16)

    @pl.loop(0, info_ref[3 + group])
    def _(step):
        for half in range(2):
            base = first + step * UNROLL + half * (UNROLL // 2)
            codes = [code_ref[base + e] for e in range(UNROLL // 2)]
            terms = [
                jnp.dot(b_ref[jnp.bitwise_and(code, 511)], placed(code), preferred_element_type=F32)
                for code in codes
            ]
            for code, term in zip(codes, terms):
                d = jnp.right_shift(code, 18)
                acc[d] = acc[d] + term

    @pl.loop(0, KP // 2)
    def _(m):
        for p in range(2):
            first_of = p * KC + 2 * m
            for o in range(8):
                rows = slice(o * 8, (o + 1) * 8)
                tile = jnp.concatenate([acc[first_of, rows], acc[first_of + 1, rows]], axis=0)
                far = jnp.bitwise_xor(yl, o // 2)
                seat = o // 2 if p == 0 else 2 * jnp.bitwise_and(far, 1) + jnp.right_shift(far, 1)
                place = (jnp.bitwise_xor(core, o % 2), p, seat, m)
                for earlier in before:
                    tile = tile + earlier[place].astype(F32)
                out_ref[place] = tile.astype(BF16)


def panel_sums(group, code, info, chunks, b, before=()):
    smem = pl.BlockSpec(memory_space=pltpu.SMEM)
    vmem = pl.BlockSpec(memory_space=pltpu.VMEM)
    anyw = pl.BlockSpec(memory_space=pl.ANY)
    pairs = sum(c.shape[0] for c in chunks)
    return pl.pallas_call(
        functools.partial(sum_kernel, group, len(chunks), len(before)),
        in_specs=[smem, smem] + [anyw] * len(chunks) + [vmem] * (1 + len(before)),
        out_specs=vmem,
        out_shape=jax.ShapeDtypeStruct((2, 2, NY, KP // 2, 16, 2 * T), BF16),
        scratch_shapes=[
            pltpu.VMEM((pairs, T, 2 * T), BF16),
            pltpu.VMEM((2 * KC + 1, T, 2 * T), F32),
            pltpu.SemaphoreType.DMA((len(chunks),)),
        ],
        compiler_params=pltpu.CompilerParams(vmem_limit_bytes=24 * MIB),
        cost_estimate=pl.CostEstimate(flops=pairs * 2**20, bytes_accessed=8 * MIB, transcendentals=0),
        name=f"panel_sums_{group}",
    )(code, info, *chunks, b, *before)


def body(a_tiles, a_cols, a_count, a_slot, agg, p_tiles):
    rows, slots = a_tiles.shape[:2]
    total = rows * slots
    core, yl, me_x = lax.axis_index("core"), lax.axis_index("yl"), lax.axis_index("x")
    packed = jnp.concatenate([p_tiles[0, :4], p_tiles[0, 4:]], axis=-1)

    live = jnp.arange(slots, dtype=I32)[None, :] < a_count
    owner = a_cols // 8
    far = jnp.bitwise_and(owner - me_x + 4, 3)
    high = (owner // 4) % 2
    group = jnp.where(far == 0, 0, jnp.where(far == 2, 2, jnp.where((far == 3) == (high == 0), 0, 1)))
    seat = jnp.where(far == 1, 3 - 2 * (1 - high), jnp.where(far == 3, 2 * (1 - high), high))
    pair = seat * 32 + owner // 8 * 4 + a_cols % 4
    to_high = jnp.broadcast_to(agg[:, None] % CR, a_cols.shape)
    target = agg[:, None] // CR * KC + a_slot
    swap = ((a_cols % 8) // 4 + to_high) % 2
    code = ((target * 2 + to_high) * 2 + swap) * 2**16 + pair * 2**9 + jnp.arange(total, dtype=I32).reshape(rows, slots)
    code = code.reshape(total)
    picked = (group.reshape(total)[:, None] == jnp.arange(3, dtype=I32)) & live.reshape(total)[:, None]
    lower = jnp.arange(total, dtype=I32)[:, None] > jnp.arange(total, dtype=I32)[None, :]
    rank = jnp.dot(lower.astype(BF16), picked.astype(BF16), preferred_element_type=F32).astype(I32)
    steps = (jnp.sum(picked.astype(I32), axis=0) + UNROLL - 1) // UNROLL
    first = (jnp.cumsum(steps) - steps) * UNROLL
    place = jnp.sum(jnp.where(picked, rank + first[None, :] + 1, 0), axis=1) - 1
    here = jnp.arange(total + 3 * UNROLL, dtype=I32)[:, None] == place[None, :]
    empty = 2 * KC * 2**18
    code = jnp.sum(jnp.where(here, code[None, :] - empty, 0), axis=1) + empty
    info = jnp.concatenate([first, steps, jnp.stack([core, yl])]).astype(I32)

    column = spread(packed, ("yh", "z")).reshape(-1, T, 2 * T)
    column, packed, info, code = lax.optimization_barrier((column, packed, info, code))
    low, high = column[:column.shape[0] // 2], column[column.shape[0] // 2:]
    left_a, right_b = shifted(low, "x", 1), shifted(high, "x", -1)
    left_b, right_a = shifted(high, "x", 1), shifted(low, "x", -1)
    left2, right2 = shifted(left_a, "x", 1), shifted(right_b, "x", -1)

    b = left_products(spread(packed, COL), a_tiles)
    sums0 = panel_sums(0, code, info, [column, left_a, right_b], b)
    sums1 = panel_sums(1, code, info, [left_b, right_a], b)
    sums2 = panel_sums(2, code, info, [left2, right2], b, (sums0, sums1))

    swap_in = swapped(sums2[1], "core", 1)
    staying, coming = [(sums2[0, p].astype(F32) + swap_in[p].astype(F32)).astype(BF16) for p in range(2)]
    staying = lax.all_to_all(staying, "yl", 0, 0, tiled=True)
    two = coming[:2].astype(F32) + swapped(coming[2:], "yl", 1).astype(F32)
    count = lax.axis_size(ROW)
    ahead = [[(r * NY + y, (r + 1) % count * NY + (y ^ by)) for r in range(count) for y in range(NY)] for by in (0, 2)]
    last = [lax.ppermute(two[n].astype(BF16), ROW + ("yl",), ahead[n]) for n in range(2)]
    result = jnp.sum(staying.astype(F32), axis=0) + sum(part.astype(F32) for part in last)
    result = result.reshape(KP, 8, 2 * T)[:KC]
    return jnp.stack([result[..., :T], result[..., T:]])


def solution(mesh):
    fine = Mesh(mesh.devices.reshape(8, 2, 4, 4, 2), ROW + COL)
    return jax.shard_map(
        body,
        mesh=fine,
        in_specs=(
            P(ROW, COL, None, None),
            P(ROW, COL),
            P(ROW, COL),
            P(ROW, COL),
            P(ROW),
            P(COL, ROW, None, None),
        ),
        out_specs=P(ROW, None, COL, None),
        check_vma=False,
    )
```

```python
import functools

import jax
import jax.numpy as jnp
from jax import lax
from jax.experimental import pallas as pl
from jax.experimental.pallas import tpu as pltpu
from jax.sharding import Mesh, PartitionSpec as P

KC = 27
CR = 2
T = 64
NY = 4
ROW = ("z", "yh", "x")
COL = ("yl", "core")
UNROLL = 8
F32 = jnp.float32
BF16 = jnp.bfloat16
I32 = jnp.int32
MIB = 2**20


def shifted(value, axis, by):
    count = lax.axis_size(axis)
    return lax.ppermute(value, axis, [(i, (i + by) % count) for i in range(count)])


def swapped(value, axis, by):
    return lax.ppermute(value, axis, [(i, i ^ by) for i in range(lax.axis_size(axis))])


def spread(value, axis):
    count = lax.axis_size(axis)
    copies = jnp.broadcast_to(value[None], (count,) + value.shape)
    return lax.all_to_all(copies, axis, 0, 0, tiled=True)


def left_kernel(own_ref, a_ref, b_ref, a_here, sems):
    def fetch(v, h):
        return pltpu.make_async_copy(a_ref.at[h, v], a_here.at[v, h], sems.at[v, h])

    for v in range(4):
        for h in range(2):
            fetch(v, h).start()

    @pl.loop(0, 4)
    def _(v):
        for h in range(2):
            fetch(v, h).wait()
        for c in range(8):
            both = own_ref[c, v].astype(F32).T.astype(BF16)
            for h in range(2):
                left = both[h * T:(h + 1) * T]
                for s in range(a_ref.shape[3]):
                    b_ref[h, v, c, s] = jnp.dot(left, a_here[v, h, c, s], preferred_element_type=F32).astype(BF16)


def left_products(own, a_tiles):
    rows, slots = a_tiles.shape[:2]
    a = a_tiles.reshape(2, 4, 8, slots, T, T)
    vmem = pl.BlockSpec(memory_space=pltpu.VMEM)
    b = pl.pallas_call(
        left_kernel,
        in_specs=[vmem, pl.BlockSpec(memory_space=pltpu.HBM)],
        out_specs=vmem,
        out_shape=jax.ShapeDtypeStruct(a.shape, BF16),
        scratch_shapes=[pltpu.VMEM((4, 2, 8, slots, T, T), BF16), pltpu.SemaphoreType.DMA((4, 2))],
        compiler_params=pltpu.CompilerParams(vmem_limit_bytes=46 * MIB),
        cost_estimate=pl.CostEstimate(flops=2 * rows * slots * T**3, bytes_accessed=16 * MIB, transcendentals=0),
        name="left_products",
    )(own, a)
    return b.reshape(rows * slots, T, T)


def sum_kernel(group, n_chunks, n_before, *refs):
    code_ref, info_ref = refs[:2]
    chunks = refs[2:2 + n_chunks]
    b_ref = refs[2 + n_chunks]
    before = refs[3 + n_chunks:3 + n_chunks + n_before]
    out_ref, panel, acc, sems = refs[-4:]
    core = info_ref[6]
    copies, at = [], 0
    for n, chunk in enumerate(chunks):
        size = chunk.shape[0]
        copies.append(pltpu.make_async_copy(chunk, panel.at[pl.ds(at, size)], sems.at[n]))
        at += size
    for copy in copies:
        copy.start()

    @pl.loop(0, acc.shape[0])
    def _(d):
        acc[d] = jnp.zeros((T, 2 * T), F32)

    for copy in copies:
        copy.wait()
    first = info_ref[group]
    low = lax.broadcasted_iota(I32, (T, 2 * T), 1) < T

    def placed(code):
        pairs = panel[jnp.bitwise_and(jnp.right_shift(code, 9), 127)].astype(F32)
        swap = jnp.bitwise_and(jnp.right_shift(code, 16), 1) == 1
        to_low = jnp.bitwise_and(jnp.right_shift(code, 17), 1) == 0
        pairs = jnp.where(swap, pltpu.roll(pairs, T, 1), pairs)
        return jnp.where(low == to_low, pairs, 0.0).astype(BF16)

    @pl.loop(0, info_ref[3 + group])
    def _(step):
        for half in range(2):
            base = first + step * UNROLL + half * (UNROLL // 2)
            codes = [code_ref[base + e] for e in range(UNROLL // 2)]
            terms = [
                jnp.dot(b_ref[jnp.bitwise_and(code, 511)], placed(code), preferred_element_type=F32)
                for code in codes
            ]
            for code, term in zip(codes, terms):
                d = jnp.right_shift(code, 18)
                acc[d] = acc[d] + term

    @pl.loop(0, KC)
    def _(k):
        for o in range(8):
            tile = jnp.concatenate([acc[k, o * 8:(o + 1) * 8], acc[KC + k, o * 8:(o + 1) * 8]], axis=0)
            place = (jnp.bitwise_xor(core, o % 2), o // 4, o // 2 % 2, k)
            for earlier in before:
                tile = tile + earlier[place].astype(F32)
            out_ref[place] = tile.astype(BF16)


def panel_sums(group, code, info, chunks, b, before=()):
    smem = pl.BlockSpec(memory_space=pltpu.SMEM)
    vmem = pl.BlockSpec(memory_space=pltpu.VMEM)
    anyw = pl.BlockSpec(memory_space=pl.ANY)
    pairs = sum(c.shape[0] for c in chunks)
    return pl.pallas_call(
        functools.partial(sum_kernel, group, len(chunks), len(before)),
        in_specs=[smem, smem] + [anyw] * len(chunks) + [vmem] * (1 + len(before)),
        out_specs=vmem,
        out_shape=jax.ShapeDtypeStruct((2, 2, 2, KC, 16, 2 * T), BF16),
        scratch_shapes=[
            pltpu.VMEM((pairs, T, 2 * T), BF16),
            pltpu.VMEM((2 * KC + 1, T, 2 * T), F32),
            pltpu.SemaphoreType.DMA((len(chunks),)),
        ],
        compiler_params=pltpu.CompilerParams(vmem_limit_bytes=24 * MIB),
        cost_estimate=pl.CostEstimate(flops=pairs * 2**20, bytes_accessed=8 * MIB, transcendentals=0),
        name=f"panel_sums_{group}",
    )(code, info, *chunks, b, *before)


def body(a_tiles, a_cols, a_count, a_slot, agg, p_tiles):
    rows, slots = a_tiles.shape[:2]
    total = rows * slots
    core, yl, me_x = lax.axis_index("core"), lax.axis_index("yl"), lax.axis_index("x")
    packed = jnp.concatenate([p_tiles[0, :4], p_tiles[0, 4:]], axis=-1)

    live = jnp.arange(slots, dtype=I32)[None, :] < a_count
    owner = a_cols // 8
    far = jnp.bitwise_and(owner - me_x + 4, 3)
    high = (owner // 4) % 2
    group = jnp.where(far == 0, 0, jnp.where(far == 2, 2, jnp.where((far == 3) == (high == 0), 0, 1)))
    seat = jnp.where(far == 1, 3 - 2 * (1 - high), jnp.where(far == 3, 2 * (1 - high), high))
    pair = seat * 32 + owner // 8 * 4 + a_cols % 4
    to_high = jnp.broadcast_to(agg[:, None] % CR, a_cols.shape)
    target = agg[:, None] // CR * KC + a_slot
    swap = ((a_cols % 8) // 4 + to_high) % 2
    code = ((target * 2 + to_high) * 2 + swap) * 2**16 + pair * 2**9 + jnp.arange(total, dtype=I32).reshape(rows, slots)
    code = code.reshape(total)
    picked = (group.reshape(total)[:, None] == jnp.arange(3, dtype=I32)) & live.reshape(total)[:, None]
    lower = jnp.arange(total, dtype=I32)[:, None] > jnp.arange(total, dtype=I32)[None, :]
    rank = jnp.dot(lower.astype(BF16), picked.astype(BF16), preferred_element_type=F32).astype(I32)
    steps = (jnp.sum(picked.astype(I32), axis=0) + UNROLL - 1) // UNROLL
    first = (jnp.cumsum(steps) - steps) * UNROLL
    place = jnp.sum(jnp.where(picked, rank + first[None, :] + 1, 0), axis=1) - 1
    here = jnp.arange(total + 3 * UNROLL, dtype=I32)[:, None] == place[None, :]
    empty = 2 * KC * 2**18
    code = jnp.sum(jnp.where(here, code[None, :] - empty, 0), axis=1) + empty
    info = jnp.concatenate([first, steps, jnp.stack([core, yl])]).astype(I32)

    column = spread(packed, ("yh", "z")).reshape(-1, T, 2 * T)
    column, packed, info, code = lax.optimization_barrier((column, packed, info, code))
    low, high = column[:column.shape[0] // 2], column[column.shape[0] // 2:]
    left_a, right_b = shifted(low, "x", 1), shifted(high, "x", -1)
    left_b, right_a = shifted(high, "x", 1), shifted(low, "x", -1)
    left2, right2 = shifted(left_a, "x", 1), shifted(right_b, "x", -1)

    b = left_products(spread(packed, COL), a_tiles)
    sums0 = panel_sums(0, code, info, [column, left_a, right_b], b)
    sums1 = panel_sums(1, code, info, [left_b, right_a], b)
    sums2 = panel_sums(2, code, info, [left2, right2], b, (sums0, sums1))

    chip = sums2[0].astype(F32) + swapped(sums2[1], "core", 1).astype(F32)
    staying = chip[..., :8, :].astype(BF16).reshape(NY, KC, 8, 2 * T)
    staying = lax.all_to_all(staying, "yl", 0, 0, tiled=True)
    coming = chip[..., 8:, :].astype(BF16)
    bit0, bit1 = yl % 2, yl // 2
    pick = functools.partial(lax.dynamic_index_in_dim, keepdims=False)
    two = pick(coming, bit0, 1).astype(F32) + swapped(pick(coming, 1 - bit0, 1), "yl", 1).astype(F32)
    count = lax.axis_size(ROW)
    ahead = [[(r * NY + y, (r + 1) % count * NY + (y ^ by)) for r in range(count) for y in range(NY)] for by in (0, 2)]
    last = [
        lax.ppermute(pick(two, 1 - bit1, 0).astype(BF16), ROW + ("yl",), ahead[1]),
        lax.ppermute(pick(two, bit1, 0).astype(BF16), ROW + ("yl",), ahead[0]),
    ]
    result = jnp.sum(staying.astype(F32), axis=0) + sum(part.astype(F32) for part in last)
    return jnp.stack([result[..., :T], result[..., T:]])


def solution(mesh):
    fine = Mesh(mesh.devices.reshape(8, 2, 4, 4, 2), ROW + COL)
    return jax.shard_map(
        body,
        mesh=fine,
        in_specs=(
            P(ROW, COL, None, None),
            P(ROW, COL),
            P(ROW, COL),
            P(ROW, COL),
            P(ROW),
            P(COL, ROW, None, None),
        ),
        out_specs=P(ROW, None, COL, None),
        check_vma=False,
    )
```

```python
import functools

import jax
import jax.numpy as jnp
from jax import lax
from jax.experimental import pallas as pl
from jax.experimental.pallas import tpu as pltpu
from jax.sharding import Mesh, PartitionSpec as P

KC = 27
CR = 2
T = 64
NY = 4
ROW = ("z", "yh", "x")
COL = ("yl", "core")
UNROLL = 8
F32 = jnp.float32
BF16 = jnp.bfloat16
I32 = jnp.int32
MIB = 2**20


def shifted(value, axis, by):
    count = lax.axis_size(axis)
    return lax.ppermute(value, axis, [(i, (i + by) % count) for i in range(count)])


def swapped(value, axis, by):
    return lax.ppermute(value, axis, [(i, i ^ by) for i in range(lax.axis_size(axis))])


def spread(value, axis):
    count = lax.axis_size(axis)
    copies = jnp.broadcast_to(value[None], (count,) + value.shape)
    return lax.all_to_all(copies, axis, 0, 0, tiled=True)


def left_kernel(own_ref, a_ref, b_ref, a_here, sems):
    def fetch(v, h):
        return pltpu.make_async_copy(a_ref.at[h, v], a_here.at[v, h], sems.at[v, h])

    for v in range(4):
        for h in range(2):
            fetch(v, h).start()

    @pl.loop(0, 4)
    def _(v):
        for h in range(2):
            fetch(v, h).wait()
        for c in range(8):
            both = own_ref[c, v].astype(F32).T.astype(BF16)
            for h in range(2):
                left = both[h * T:(h + 1) * T]
                for s in range(a_ref.shape[3]):
                    b_ref[h, v, c, s] = jnp.dot(left, a_here[v, h, c, s], preferred_element_type=F32).astype(BF16)


def left_products(own, a_tiles):
    rows, slots = a_tiles.shape[:2]
    a = a_tiles.reshape(2, 4, 8, slots, T, T)
    vmem = pl.BlockSpec(memory_space=pltpu.VMEM)
    b = pl.pallas_call(
        left_kernel,
        in_specs=[vmem, pl.BlockSpec(memory_space=pltpu.HBM)],
        out_specs=vmem,
        out_shape=jax.ShapeDtypeStruct(a.shape, BF16),
        scratch_shapes=[pltpu.VMEM((4, 2, 8, slots, T, T), BF16), pltpu.SemaphoreType.DMA((4, 2))],
        compiler_params=pltpu.CompilerParams(vmem_limit_bytes=46 * MIB),
        cost_estimate=pl.CostEstimate(flops=2 * rows * slots * T**3, bytes_accessed=16 * MIB, transcendentals=0),
        name="left_products",
    )(own, a)
    return b.reshape(rows * slots, T, T)


def sum_kernel(group, n_chunks, n_before, *refs):
    code_ref, info_ref = refs[:2]
    chunks = refs[2:2 + n_chunks]
    b_ref = refs[2 + n_chunks]
    before = refs[3 + n_chunks:3 + n_chunks + n_before]
    out_ref, panel, acc, sems = refs[-4:]
    core = info_ref[6]
    copies, at = [], 0
    for n, chunk in enumerate(chunks):
        size = chunk.shape[0]
        copies.append(pltpu.make_async_copy(chunk, panel.at[pl.ds(at, size)], sems.at[n]))
        at += size
    for copy in copies:
        copy.start()

    @pl.loop(0, acc.shape[0])
    def _(d):
        acc[d] = jnp.zeros((T, 2 * T), F32)

    for copy in copies:
        copy.wait()
    first = info_ref[group]
    low = lax.broadcasted_iota(I32, (T, 2 * T), 1) < T

    def placed(code):
        pairs = panel[jnp.bitwise_and(jnp.right_shift(code, 9), 127)].astype(F32)
        swap = jnp.bitwise_and(jnp.right_shift(code, 16), 1) == 1
        to_low = jnp.bitwise_and(jnp.right_shift(code, 17), 1) == 0
        pairs = jnp.where(swap, pltpu.roll(pairs, T, 1), pairs)
        return jnp.where(low == to_low, pairs, 0.0).astype(BF16)

    @pl.loop(0, info_ref[3 + group])
    def _(step):
        for half in range(2):
            base = first + step * UNROLL + half * (UNROLL // 2)
            codes = [code_ref[base + e] for e in range(UNROLL // 2)]
            terms = [
                jnp.dot(b_ref[jnp.bitwise_and(code, 511)], placed(code), preferred_element_type=F32)
                for code in codes
            ]
            for code, term in zip(codes, terms):
                d = jnp.right_shift(code, 18)
                acc[d] = acc[d] + term

    @pl.loop(0, KC)
    def _(k):
        for o in range(8):
            tile = jnp.concatenate([acc[k, o * 8:(o + 1) * 8], acc[KC + k, o * 8:(o + 1) * 8]], axis=0)
            place = (jnp.bitwise_xor(core, o % 2), o // 4, o // 2 % 2, k)
            for earlier in before:
                tile = tile + earlier[place].astype(F32)
            out_ref[place] = tile.astype(BF16)


def panel_sums(group, code, info, chunks, b, before=()):
    smem = pl.BlockSpec(memory_space=pltpu.SMEM)
    vmem = pl.BlockSpec(memory_space=pltpu.VMEM)
    anyw = pl.BlockSpec(memory_space=pl.ANY)
    pairs = sum(c.shape[0] for c in chunks)
    return pl.pallas_call(
        functools.partial(sum_kernel, group, len(chunks), len(before)),
        in_specs=[smem, smem] + [anyw] * len(chunks) + [vmem] * (1 + len(before)),
        out_specs=vmem,
        out_shape=jax.ShapeDtypeStruct((2, 2, 2, KC, 16, 2 * T), BF16),
        scratch_shapes=[
            pltpu.VMEM((pairs, T, 2 * T), BF16),
            pltpu.VMEM((2 * KC + 1, T, 2 * T), F32),
            pltpu.SemaphoreType.DMA((len(chunks),)),
        ],
        compiler_params=pltpu.CompilerParams(vmem_limit_bytes=24 * MIB),
        cost_estimate=pl.CostEstimate(flops=pairs * 2**20, bytes_accessed=8 * MIB, transcendentals=0),
        name=f"panel_sums_{group}",
    )(code, info, *chunks, b, *before)


def body(a_tiles, a_cols, a_count, a_slot, agg, p_tiles):
    rows, slots = a_tiles.shape[:2]
    total = rows * slots
    core, yl, me_x = lax.axis_index("core"), lax.axis_index("yl"), lax.axis_index("x")
    packed = jnp.concatenate([p_tiles[0, :4], p_tiles[0, 4:]], axis=-1)

    live = jnp.arange(slots, dtype=I32)[None, :] < a_count
    owner = a_cols // 8
    far = jnp.bitwise_and(owner - me_x + 4, 3)
    high = (owner // 4) % 2
    group = jnp.where(far == 0, 0, jnp.where(far == 2, 2, jnp.where((far == 3) == (high == 0), 0, 1)))
    seat = jnp.where(far == 1, 3 - 2 * (1 - high), jnp.where(far == 3, 2 * (1 - high), high))
    pair = seat * 32 + owner // 8 * 4 + a_cols % 4
    to_high = jnp.broadcast_to(agg[:, None] % CR, a_cols.shape)
    target = agg[:, None] // CR * KC + a_slot
    swap = ((a_cols % 8) // 4 + to_high) % 2
    code = ((target * 2 + to_high) * 2 + swap) * 2**16 + pair * 2**9 + jnp.arange(total, dtype=I32).reshape(rows, slots)
    code = code.reshape(total)
    picked = (group.reshape(total)[:, None] == jnp.arange(3, dtype=I32)) & live.reshape(total)[:, None]
    lower = jnp.arange(total, dtype=I32)[:, None] > jnp.arange(total, dtype=I32)[None, :]
    rank = jnp.dot(lower.astype(BF16), picked.astype(BF16), preferred_element_type=F32).astype(I32)
    steps = (jnp.sum(picked.astype(I32), axis=0) + UNROLL - 1) // UNROLL
    first = (jnp.cumsum(steps) - steps) * UNROLL
    place = jnp.sum(jnp.where(picked, rank + first[None, :] + 1, 0), axis=1) - 1
    here = jnp.arange(total + 3 * UNROLL, dtype=I32)[:, None] == place[None, :]
    empty = 2 * KC * 2**18
    code = jnp.sum(jnp.where(here, code[None, :] - empty, 0), axis=1) + empty
    info = jnp.concatenate([first, steps, jnp.stack([core, yl])]).astype(I32)

    column = spread(packed, ("yh", "z")).reshape(-1, T, 2 * T)
    column, packed, info, code = lax.optimization_barrier((column, packed, info, code))
    low, high = column[:column.shape[0] // 2], column[column.shape[0] // 2:]
    left_a, right_b = shifted(low, "x", 1), shifted(high, "x", -1)
    left_b, right_a = shifted(high, "x", 1), shifted(low, "x", -1)
    left2, right2 = shifted(left_a, "x", 1), shifted(right_b, "x", -1)

    b = left_products(spread(packed, COL), a_tiles)
    sums0 = panel_sums(0, code, info, [column, left_a, right_b], b)
    sums1 = panel_sums(1, code, info, [left_b, right_a], b, (sums0,))
    sums2 = panel_sums(2, code, info, [left2, right2], b, (sums1,))

    chip = sums2[0].astype(F32) + swapped(sums2[1], "core", 1).astype(F32)
    staying = chip[..., :8, :].astype(BF16).reshape(NY, KC, 8, 2 * T)
    staying = lax.all_to_all(staying, "yl", 0, 0, tiled=True)
    coming = chip[..., 8:, :].astype(BF16)
    bit0, bit1 = yl % 2, yl // 2
    pick = functools.partial(lax.dynamic_index_in_dim, keepdims=False)
    two = pick(coming, bit0, 1).astype(F32) + swapped(pick(coming, 1 - bit0, 1), "yl", 1).astype(F32)
    count = lax.axis_size(ROW)
    ahead = [[(r * NY + y, (r + 1) % count * NY + (y ^ by)) for r in range(count) for y in range(NY)] for by in (0, 2)]
    last = [
        lax.ppermute(pick(two, bit1, 0).astype(BF16), ROW + ("yl",), ahead[0]),
        lax.ppermute(pick(two, 1 - bit1, 0).astype(BF16), ROW + ("yl",), ahead[1]),
    ]
    result = jnp.sum(staying.astype(F32), axis=0) + sum(part.astype(F32) for part in last)
    return jnp.stack([result[..., :T], result[..., T:]])


def solution(mesh):
    fine = Mesh(mesh.devices.reshape(8, 2, 4, 4, 2), ROW + COL)
    return jax.shard_map(
        body,
        mesh=fine,
        in_specs=(
            P(ROW, COL, None, None),
            P(ROW, COL),
            P(ROW, COL),
            P(ROW, COL),
            P(ROW),
            P(COL, ROW, None, None),
        ),
        out_specs=P(ROW, None, COL, None),
        check_vma=False,
    )
```
